32 devices in a mesh: slot: 4 (over z), ctx: 2 (over x), tp: 4 (over y, core).
Axes of the slice: x: 2, y: 2, z: 4, core: 2. Of those that a mesh axis runs over, the one named last changes fastest.
Arguments:
- inputs: bfloat16 [4, 1024, 2048], P('slot', 'ctx'), may hold values from -6 to 6
- lengths: int32 [4], P('slot'), may hold values from 256 to 1024, as said below
- ln_gain: float32 [2, 2048], replicated, may hold values from 0.5 to 1.5
- ln_shift: float32 [2, 2048], replicated, may hold values from -3 to 3
- w_qkv: bfloat16 [2, 3, 2048, 2048], P(None, None, ('slot', 'ctx'), 'tp'), may hold values from -0.125 to 0.125
- b_qkv: float32 [2, 3, 2048], P(None, None, 'tp'), may hold values from -2 to 2
- w_out: bfloat16 [2, 2048, 2048], P(None, 'tp', ('slot', 'ctx')), may hold values from -0.75 to 0.75
- b_out: float32 [2, 2048], replicated, may hold values from -2 to 2
- w_up: bfloat16 [2, 2048, 8192], P(None, ('slot', 'ctx'), 'tp'), may hold values from -0.125 to 0.125
- b_up: float32 [2, 8192], P(None, 'tp'), may hold values from -3 to 3
- w_down: bfloat16 [2, 8192, 2048], P(None, 'tp', ('slot', 'ctx')), may hold values from -0.0625 to 0.0625
- b_down: float32 [2, 2048], replicated, may hold values from -2 to 2
- cotangent: bfloat16 [4, 1024, 2048], P('slot', 'ctx'), may hold values from -6 to 6
Outputs:
- block_out: bfloat16 [4, 1024, 2048], P('slot', 'ctx')
- grad_input: bfloat16 [4, 1024, 2048], P('slot', 'ctx')
- grad_ln_gain: float32 [2, 2048], replicated
- grad_ln_shift: float32 [2, 2048], replicated
- grad_w_qkv: float32 [2, 3, 2048, 2048], P(None, None, ('slot', 'ctx'), 'tp')
- grad_b_qkv: float32 [2, 3, 2048], P(None, None, 'tp')
- grad_w_out: float32 [2, 2048, 2048], P(None, 'tp', ('slot', 'ctx'))
- grad_b_out: float32 [2, 2048], replicated
- grad_w_up: float32 [2, 2048, 8192], P(None, ('slot', 'ctx'), 'tp')
- grad_b_up: float32 [2, 8192], P(None, 'tp')
- grad_w_down: float32 [2, 8192, 2048], P(None, 'tp', ('slot', 'ctx'))
- grad_b_down: float32 [2, 2048], replicated
The draws below stay inside these ranges and needn't reach their ends.
Inputs may be any that keep to these rules, and one draw needn't show every extreme that they name: `lengths`: valid positions of a slot are a prefix of it; in every draw one slot, drawn from the seed, is full.
All inputs are finite; a program needn't handle non-finite values.
Results may differ from the reference program's by a relative error of at most 0.033.
Values may be sent and summed in bfloat16 or wider, within the bound.
No kernel may reach another device: no remote copies, remote signals or barrier semaphores. Data moves between devices by JAX's collectives and lax.ppermute only.
A program may use at most 320 MiB of HBM per device.

```python
import math
import jax
import jax.numpy as jnp
from jax import lax

D = 2048
HEADS = 32
HD = 64
ROT = 32
FF = 8192
LAYERS = 2
SLOTS = 4
SLOT_LEN = 1024


def draw_lengths(key, part):
    key = jax.random.fold_in(key, 7)
    base_key, pick_key = jax.random.split(key)
    drawn = jax.random.randint(base_key, (SLOTS,), SLOT_LEN // 4, SLOT_LEN + 1, dtype=jnp.int32)
    chosen = jax.random.randint(pick_key, (), 0, SLOTS, dtype=jnp.int32)
    return jnp.where(jnp.arange(SLOTS, dtype=jnp.int32) == chosen, SLOT_LEN, drawn).astype(jnp.int32)


def block_levels(rng, dims, cuts, smallest, high):
    loudness = 1.0
    for dim, parts in cuts:
        draws = jax.random.uniform(jax.random.fold_in(jax.random.fold_in(rng, 6), dim), (parts,), jnp.float32, smallest / len(cuts), high / len(cuts))
        loudness = loudness * jnp.repeat(jnp.exp(draws), dims[dim] // parts).reshape((-1,) + (1,) * (len(dims) - 1 - dim))
    return loudness


def gaussian(rng, shape, scale, most, cuts=(), kind=jnp.bfloat16):
    loudness = block_levels(rng, shape, cuts, -0.22, 0.18) if cuts else 1.0
    entries = jax.random.normal(rng, shape, jnp.float32) * scale * loudness
    return jnp.minimum(jnp.maximum(entries, -most), most).astype(kind)


def setup_inputs(seed: int = 0) -> dict:
    arg_keys = jax.random.split(jax.random.key(seed), 14)
    return {
        "inputs": gaussian(arg_keys[0], (SLOTS, SLOT_LEN, D), 1.0, 6.0, ((0, 4), (1, 2))),
        "lengths": draw_lengths(jax.random.fold_in(arg_keys[13], 71), 0),
        "ln_gain": jnp.clip(1.0 + 0.1 * jax.random.normal(arg_keys[2], (LAYERS, D), jnp.float32), 0.5, 1.5),
        "ln_shift": gaussian(arg_keys[3], (LAYERS, D), 0.5, 3.0, (), jnp.float32),
        "w_qkv": gaussian(arg_keys[4], (LAYERS, 3, D, D), D ** -0.5, 0.125, ((2, 8), (3, 4))),
        "b_qkv": gaussian(arg_keys[5], (LAYERS, 3, D), 0.3, 2.0, ((2, 4),), jnp.float32),
        "w_out": gaussian(arg_keys[6], (LAYERS, D, D), (D // 32) ** -0.5, 0.75, ((1, 4), (2, 8))),
        "b_out": gaussian(arg_keys[7], (LAYERS, D), 0.3, 2.0, (), jnp.float32),
        "w_up": gaussian(arg_keys[8], (LAYERS, D, FF), D ** -0.5, 0.125, ((1, 8), (2, 4))),
        "b_up": gaussian(arg_keys[9], (LAYERS, FF), 0.5, 3.0, ((1, 4),), jnp.float32),
        "w_down": gaussian(arg_keys[10], (LAYERS, FF, D), FF ** -0.5, 0.0625, ((1, 4), (2, 8))),
        "b_down": gaussian(arg_keys[11], (LAYERS, D), 0.3, 2.0, (), jnp.float32),
        "cotangent": gaussian(arg_keys[12], (SLOTS, SLOT_LEN, D), 1.0, 6.0, ((0, 4), (1, 2))),
    }


@jax.custom_vjp
def low(v):
    return lax.optimization_barrier(v.astype(jnp.bfloat16)).astype(jnp.float32)

@jax.custom_vjp
def low_back(v):
    return v

def low_keep(v):
    return (low(v), None)

def low_pass(kept, grad):
    return (grad,)

def back_keep(v):
    return (v, None)

def back_low(kept, grad):
    return (low(grad),)
low.defvjp(low_keep, low_pass)
low_back.defvjp(back_keep, back_low)
highest = lax.Precision.HIGHEST
masked = -1e+30

def layer_norm(hidden, gain, shift):
    centre = lax.optimization_barrier(jnp.mean(hidden, -1, keepdims=True))
    centred = hidden - centre
    variance = lax.optimization_barrier(jnp.mean(centred * centred, -1, keepdims=True))
    return centred * lax.rsqrt(variance + 1e-05) * gain + shift

def gelu_tanh(value):
    inner = 0.7978845608028654 * (value + 0.044715 * value * value * value)
    return 0.5 * value * (1.0 + jnp.tanh(inner))

def rotary_tables(positions):
    half_rot = ROT // 2
    freqs = jnp.exp(jnp.arange(half_rot, dtype=jnp.float32) * (-2.0 * math.log(10000.0) / ROT))
    angles = positions.astype(jnp.float32)[:, None] * freqs[None, :]
    return (jnp.cos(angles), jnp.sin(angles))

def rotate(tensor, cosine, sine):
    half_rot = ROT // 2
    lead_part = tensor[..., :half_rot]
    tail_part = tensor[..., half_rot:ROT]
    remain_part = tensor[..., ROT:]
    cos_rows = cosine[:, None, :]
    sin_rows = sine[:, None, :]
    return jnp.concatenate([lead_part * cos_rows - tail_part * sin_rows, tail_part * cos_rows + lead_part * sin_rows, remain_part], axis=-1)

def attend_slot(query, keys, values, length):
    block = math.gcd(512, SLOT_LEN)
    count = SLOT_LEN // block
    key_pos = jnp.arange(SLOT_LEN, dtype=jnp.int32)
    blocks = query.reshape(count, block, HEADS, HD)
    starts = jnp.arange(count, dtype=jnp.int32) * block

    @jax.checkpoint
    def one_block(packed):
        rows, start = packed
        product = jnp.einsum('qhd,khd->hqk', rows, keys, precision=highest)
        scores = low_back(product) * HD ** (-0.5)
        query_pos = start + jnp.arange(block, dtype=jnp.int32)
        allowed = (key_pos[None, :] <= query_pos[:, None]) & (key_pos[None, :] < length)
        scores = jnp.where(allowed[None], scores, masked)
        row_top = lax.optimization_barrier(jnp.max(scores, -1, keepdims=True))
        logsum = row_top + jnp.log(lax.optimization_barrier(jnp.sum(jnp.exp(scores - row_top), -1, keepdims=True)))
        probs = low(jnp.exp(scores - logsum))
        return jnp.einsum('hqk,khd->qhd', probs, values, precision=highest)
    return lax.map(one_block, (blocks, starts)).reshape(SLOT_LEN, HEADS, HD)

def forward(inputs, gains, shifts, w_qkv, b_qkv, w_out, b_out, w_up, b_up, w_down, b_down, lengths):
    valid = (jnp.arange(SLOT_LEN, dtype=jnp.int32)[None, :] < lengths[:, None]).astype(jnp.float32)
    cosine, sine = rotary_tables(jnp.arange(SLOT_LEN, dtype=jnp.int32))
    hidden = inputs.reshape(SLOTS * SLOT_LEN, D)
    for layer_idx in range(LAYERS):
        normed = low(layer_norm(hidden, gains[layer_idx], shifts[layer_idx]))
        shaped = []
        for part_idx in range(3):
            linear = jnp.dot(normed, w_qkv[layer_idx, part_idx], precision=highest, preferred_element_type=jnp.float32)
            linear = low_back(linear + b_qkv[layer_idx, part_idx])
            shaped.append(linear.reshape(SLOTS, SLOT_LEN, HEADS, HD))
        query = low(rotate(shaped[0], cosine, sine))
        keys = low(rotate(shaped[1], cosine, sine))
        values = low(shaped[2])
        attended = lax.map(lambda packed: attend_slot(packed[0], packed[1], packed[2], packed[3]), (query, keys, values, lengths))
        attended = low_back(low(attended.reshape(SLOTS * SLOT_LEN, D)))
        upward = jnp.dot(normed, w_up[layer_idx], precision=highest, preferred_element_type=jnp.float32)
        upward = low_back(upward + b_up[layer_idx])
        activated = low(gelu_tanh(upward))
        branch = jnp.dot(attended, w_out[layer_idx], precision=highest, preferred_element_type=jnp.float32)
        branch = branch + jnp.dot(activated, w_down[layer_idx], precision=highest, preferred_element_type=jnp.float32)
        branch = low_back(branch)
        hidden = hidden + branch + b_out[layer_idx] + b_down[layer_idx]
    return hidden.reshape(SLOTS, SLOT_LEN, D) * valid[:, :, None]

def reference(inputs, lengths, ln_gain, ln_shift, w_qkv, b_qkv, w_out, b_out, w_up, b_up, w_down, b_down, cotangent):
    floats = [array_in.astype(jnp.float32) for array_in in (inputs, ln_gain, ln_shift, w_qkv, b_qkv, w_out, b_out, w_up, b_up, w_down, b_down)]

    def closed(*values):
        return forward(*values, lengths)
    primal, pullback = jax.vjp(closed, *floats)
    grads = pullback(cotangent.astype(jnp.float32))
    return (primal.astype(jnp.bfloat16), grads[0].astype(jnp.bfloat16), grads[1], grads[2], grads[3], grads[4], grads[5], grads[6], grads[7], grads[8], grads[9], grads[10])
```

```python
import functools
import math

import jax
import jax.numpy as jnp
from jax import lax
from jax.experimental import pallas as pl
from jax.experimental.pallas import tpu as pltpu
from jax.sharding import PartitionSpec as P

HD = 64
ROT = 32
LAYERS = 2

masked = -1e30
F32 = jnp.float32
BF16 = jnp.bfloat16
NT = (((1,), (1,)), ((), ()))
TN = (((0,), (0,)), ((), ()))
VMEM_LIMIT = 20 * 1024 * 1024


def dot(a, b, dims=None):
    if dims is None:
        return jnp.dot(a, b, preferred_element_type=F32)
    return lax.dot_general(a, b, dims, preferred_element_type=F32)


def gelu_tanh(value):
    inner = 0.7978845608028654 * (value + 0.044715 * value * value * value)
    return 0.5 * value * (1.0 + jnp.tanh(inner))


def gelu_slope(value):
    square = value * value
    inner = 0.7978845608028654 * (value + 0.044715 * value * square)
    bend = jnp.tanh(inner)
    slope = 0.7978845608028654 * (1.0 + 3.0 * 0.044715 * square)
    return 0.5 * (1.0 + bend) + 0.5 * value * (1.0 - bend * bend) * slope


def layer_norm(hidden, gain, shift):
    centre = jnp.mean(hidden, -1, keepdims=True)
    centred = hidden - centre
    variance = jnp.mean(centred * centred, -1, keepdims=True)
    return centred * lax.rsqrt(variance + 1e-05) * gain + shift


def rotary_tables(positions, heads):
    half_rot = ROT // 2
    freqs = jnp.exp(jnp.arange(half_rot, dtype=F32) * (-2.0 * math.log(10000.0) / ROT))
    angles = positions.astype(F32)[:, None] * freqs[None, :]
    cosine, sine = jnp.cos(angles), jnp.sin(angles)
    rows = positions.shape[0]
    rest = jnp.zeros((rows, HD - ROT), F32)
    none = jnp.zeros_like(sine)
    same = jnp.concatenate([cosine, cosine, rest + 1.0], axis=1)
    ahead = jnp.concatenate([-sine, none, rest], axis=1)
    behind = jnp.concatenate([none, sine, rest], axis=1)
    return jnp.stack([jnp.tile(part, (1, heads)) for part in (same, ahead, behind)])


def turn(value, tables, back=False):
    width = value.shape[1]
    half_rot = ROT // 2
    moved = (
        pltpu.roll(value, width - half_rot, 1) * tables[1] + pltpu.roll(value, half_rot, 1) * tables[2]
    )
    stay = value * tables[0]
    return stay - moved if back else stay + moved


def in_kernel(count, *refs):
    xs = refs[:count]
    w_ref, bias_ref, table_ref, q_ref, kv_ref, up_ref, act_ref = refs[count:]
    n = q_ref.shape[1]
    rows = xs[0].shape[0]
    half = count // 2
    for part in range(2):
        at = slice(part * half * rows, (part + 1) * half * rows)
        x = jnp.concatenate([ref[...] for ref in xs[part * half : (part + 1) * half]], axis=0)
        out = dot(x, w_ref[...]) + bias_ref[...]
        tables = table_ref[:, at]
        q_ref[at, :] = turn(out[:, :n], tables).astype(BF16)
        kv_ref[at, :n] = turn(out[:, n : 2 * n], tables).astype(BF16)
        kv_ref[at, n:] = out[:, 2 * n : 3 * n].astype(BF16)
        up = out[:, 3 * n :]
        up_ref[at, :] = up
        act_ref[at, :] = gelu_tanh(up).astype(BF16)


def rows_of(block, width):
    return pl.BlockSpec((block, width), lambda i: (i, 0))


def whole(*shape):
    return pl.BlockSpec(shape, lambda i: (0,) * len(shape))


def params():
    return pltpu.CompilerParams(
        dimension_semantics=("arbitrary",), vmem_limit_bytes=VMEM_LIMIT
    )


def plain():
    return pltpu.CompilerParams(vmem_limit_bytes=VMEM_LIMIT)


def cost(flops, moved=0):
    return pl.CostEstimate(
        flops=int(COST_SCALE * flops), bytes_accessed=int(moved), transcendentals=0
    )


COST_SCALE = 1.5
COST = cost(1000)


def in_project(xs, win, bias, tables, n):
    rows, width = xs[0].shape
    run = rows * len(xs)
    f = win.shape[1] - 3 * n
    shape = jax.ShapeDtypeStruct
    return pl.pallas_call(
        functools.partial(in_kernel, len(xs)),
        out_shape=[
            shape((run, n), BF16),
            shape((run, 2 * n), BF16),
            shape((run, f), F32),
            shape((run, f), BF16),
        ],
        compiler_params=plain(),
        cost_estimate=cost(2 * run * width * win.shape[1], 2 * win.size),
        name="in_project",
    )(*xs, win, bias, tables)


def diagonal(block, corner, rows_each, room):
    key = lax.broadcasted_iota(jnp.int32, (block, block), 0)
    query = lax.broadcasted_iota(jnp.int32, (1, block), 1)
    inside = corner % (block // rows_each)

    def at(row):
        return (row // rows_each ^ inside) * rows_each + row % rows_each

    return at(key) < jnp.minimum(at(query) + 1, room)


def attend_kernel(rows_each, at_ref, q_ref, own_ref, prev_ref, res_ref, att_ref, lse_ref):
    length, place, corner = at_ref[0], at_ref[1], at_ref[2]
    block, n = q_ref.shape
    heads = n // HD
    run = own_ref.shape[0]
    i = pl.program_id(0)
    flip = corner * rows_each // block
    home = i ^ flip
    first = place * run + home * block

    @pl.when(first >= length)
    def _():
        res_ref[...] = jnp.zeros_like(res_ref)
        att_ref[...] = jnp.zeros_like(att_ref)
        lse_ref[...] = jnp.zeros_like(lse_ref)

    @pl.when(first < length)
    def _():
        lane = lax.broadcasted_iota(jnp.int32, (1, n), 1)
        q = q_ref[...].astype(F32) * HD ** (-0.5)
        qs = [jnp.where(lane // HD == h, q, 0.0).astype(BF16) for h in range(heads)]

        def step(keys, values, carry, limit=None):
            out = []
            for h in range(heads):
                top, total, accum = carry[h]
                scores = dot(keys, qs[h], NT)
                if limit is not None:
                    scores = jnp.where(limit, scores, masked)
                new_top = jnp.maximum(top, jnp.max(scores, 0, keepdims=True))
                probs = jnp.exp(scores - new_top)
                shrink = jnp.exp(top - new_top)
                total = total * shrink + jnp.sum(probs, 0, keepdims=True)
                accum = accum * shrink + dot(values, probs.astype(BF16), TN)
                out.append((new_top, total, accum))
            return tuple(out)

        carry = tuple(
            (
                jnp.full((1, block), masked, F32),
                jnp.zeros((1, block), F32),
                jnp.zeros((n, block), F32),
            )
            for _ in range(heads)
        )
        inner = run // block

        def prev_step(j, carry):
            rows = pl.ds(pl.multiple_of((j % inner) * block, block), block)
            return step(prev_ref[j // inner, rows, :n], prev_ref[j // inner, rows, n:], carry)

        carry = lax.fori_loop(0, place * inner, prev_step, carry)

        def own_step(j, carry):
            rows = pl.ds(pl.multiple_of((j ^ flip) * block, block), block)
            return step(own_ref[rows, :n], own_ref[rows, n:], carry)

        carry = lax.fori_loop(0, home, own_step, carry)
        limit = diagonal(block, corner, rows_each, length - first)
        rows = pl.ds(pl.multiple_of(i * block, block), block)
        carry = step(own_ref[rows, :n], own_ref[rows, n:], carry, limit)
        parts = []
        for h in range(heads):
            top, total, accum = carry[h]
            lse_ref[h : h + 1, :] = top + jnp.log(total)
            parts.append(accum[h * HD : (h + 1) * HD] / total)
        result = jnp.concatenate(parts, axis=0).T
        res_ref[...] = result
        att_ref[...] = result.astype(BF16)


def attend(at, q, kv, prev, block, rows_each):
    run, n = q.shape
    heads = n // HD
    before = prev.shape[0]
    shape = jax.ShapeDtypeStruct
    tiles = run * (before * run + run)
    return pl.pallas_call(
        functools.partial(attend_kernel, rows_each),
        grid=(run // block,),
        in_specs=[
            pl.BlockSpec(memory_space=pltpu.SMEM),
            rows_of(block, n),
            whole(run, 2 * n),
            whole(before, run, 2 * n),
        ],
        out_specs=[
            rows_of(block, n),
            rows_of(block, n),
            pl.BlockSpec((heads, block), lambda i: (0, i)),
        ],
        out_shape=[shape((run, n), F32), shape((run, n), BF16), shape((heads, run), F32)],
        compiler_params=params(),
        cost_estimate=cost(32 * run * (before * run + run) * n),
        name="attend",
    )(at, q, kv, prev)


def out_kernel(att_ref, act_ref, w_ref, *y_refs):
    rows = y_refs[0].shape[0]
    half = len(y_refs) // 2
    for part in range(2):
        at = slice(part * half * rows, (part + 1) * half * rows)
        both = jnp.concatenate([att_ref[at, :], act_ref[at, :]], axis=1)
        out = dot(both, w_ref[...], NT).astype(BF16)
        for j in range(half):
            y_refs[part * half + j][...] = out[j * rows : (j + 1) * rows]


def out_project(att, act, wout, rows):
    count = att.shape[0] // rows
    return pl.pallas_call(
        out_kernel,
        out_shape=[jax.ShapeDtypeStruct((rows, wout.shape[0]), BF16)] * count,
        compiler_params=plain(),
        cost_estimate=cost(2 * att.shape[0] * wout.size, 2 * wout.size),
        name="out_project",
    )(att, act, wout)


def out_back_kernel(count, *refs):
    xs = refs[:count]
    w_ref, up_ref, gatt_ref, gup_ref = refs[count:]
    n = gatt_ref.shape[1]
    rows = xs[0].shape[0]
    half = count // 2
    for part in range(2):
        at = slice(part * half * rows, (part + 1) * half * rows)
        x = jnp.concatenate([ref[...] for ref in xs[part * half : (part + 1) * half]], axis=0)
        out = dot(x, w_ref[...])
        gatt_ref[at, :] = out[:, :n].astype(BF16)
        gup_ref[at, :] = (out[:, n:] * gelu_slope(up_ref[at, :])).astype(BF16)


def out_back(xs, wout, up, n):
    run, f = up.shape
    shape = jax.ShapeDtypeStruct
    return pl.pallas_call(
        functools.partial(out_back_kernel, len(xs)),
        out_shape=[shape((run, n), BF16), shape((run, f), BF16)],
        compiler_params=plain(),
        cost_estimate=cost(2 * run * wout.size, 2 * wout.size),
        name="out_back",
    )(*xs, wout, up)


def attend_back_kernel(
    rows_each, at_ref, q_ref, own_ref, prev_ref, gatt_ref, res_ref, lse_ref, table_ref,
    gq_ref, gown_ref, gprev_ref, hold_ref,
):
    length, place, corner = at_ref[0], at_ref[1], at_ref[2]
    block, n = q_ref.shape
    heads = n // HD
    run = own_ref.shape[0]
    before = prev_ref.shape[0]
    i = pl.program_id(0)
    flip = corner * rows_each // block
    home = i ^ flip
    first = place * run + home * block

    @pl.when(i == 0)
    def _():
        gown_ref[...] = jnp.zeros_like(gown_ref)
        hold_ref[...] = jnp.zeros_like(hold_ref)

    @pl.when(first >= length)
    def _():
        gq_ref[...] = jnp.zeros_like(gq_ref)

    @pl.when(first < length)
    def _():
        lane = lax.broadcasted_iota(jnp.int32, (1, n), 1)
        q, gatt = q_ref[...], gatt_ref[...]
        pick = [lane // HD == h for h in range(heads)]
        zero = jnp.zeros((), BF16)
        qs = [jnp.where(p, q, zero) for p in pick]
        gs = [jnp.where(p, gatt, zero) for p in pick]
        shared = (gatt.astype(F32) * res_ref[...]).T
        deltas = [jnp.sum(shared[h * HD : (h + 1) * HD], 0, keepdims=True) for h in range(heads)]
        sums = [lse_ref[h : h + 1, :] for h in range(heads)]
        scale = HD ** (-0.5)

        def step(keys, values, carry, limit=None):
            gkeys = gvalues = None
            out = []
            for h in range(heads):
                scores = dot(keys, qs[h], NT) * scale
                if limit is not None:
                    scores = jnp.where(limit, scores, masked)
                probs = jnp.exp(scores - sums[h])
                gprobs = dot(values, gs[h], NT)
                gscores = (probs * (gprobs - deltas[h]) * scale).astype(BF16)
                gvalue = dot(probs.astype(BF16), gs[h])
                gkey = dot(gscores, qs[h])
                gkeys = gkey if gkeys is None else gkeys + gkey
                gvalues = gvalue if gvalues is None else gvalues + gvalue
                out.append(carry[h] + dot(keys, gscores, TN))
            return tuple(out), gkeys, gvalues

        carry = tuple(jnp.zeros((n, block), F32) for _ in range(heads))
        inner = run // block

        def prev_step(j, carry):
            k, rows = j // inner, pl.ds(pl.multiple_of((j % inner) * block, block), block)
            carry, gkeys, gvalues = step(prev_ref[k, rows, :n], prev_ref[k, rows, n:], carry)
            hold_ref[k, rows, :n] += gkeys
            hold_ref[k, rows, n:] += gvalues
            return carry

        carry = lax.fori_loop(0, place * inner, prev_step, carry)

        def own_step(j, carry):
            rows = pl.ds(pl.multiple_of((j ^ flip) * block, block), block)
            carry, gkeys, gvalues = step(own_ref[rows, :n], own_ref[rows, n:], carry)
            gown_ref[rows, :n] += gkeys
            gown_ref[rows, n:] += gvalues
            return carry

        carry = lax.fori_loop(0, home, own_step, carry)
        limit = diagonal(block, corner, rows_each, length - first)
        rows = pl.ds(pl.multiple_of(i * block, block), block)
        carry, gkeys, gvalues = step(own_ref[rows, :n], own_ref[rows, n:], carry, limit)
        gown_ref[rows, :n] += gkeys
        gown_ref[rows, n:] += gvalues
        gq = jnp.concatenate([carry[h][h * HD : (h + 1) * HD] for h in range(heads)], axis=0).T
        gq_ref[...] = turn(gq, table_ref[...], back=True).astype(BF16)

    @pl.when(i == pl.num_programs(0) - 1)
    def _():
        gprev_ref[...] = hold_ref[...].astype(BF16)


def attend_back(at, q, kv, prev, gatt, res, lse, tables, block, rows_each):
    run, n = q.shape
    heads = n // HD
    before = prev.shape[0]
    shape = jax.ShapeDtypeStruct
    tiles = run * (before * run + run)
    return pl.pallas_call(
        functools.partial(attend_back_kernel, rows_each),
        grid=(run // block,),
        in_specs=[
            pl.BlockSpec(memory_space=pltpu.SMEM),
            rows_of(block, n),
            whole(run, 2 * n),
            whole(before, run, 2 * n),
            rows_of(block, n),
            rows_of(block, n),
            pl.BlockSpec((heads, block), lambda i: (0, i)),
            pl.BlockSpec((3, block, n), lambda i: (0, i, 0)),
        ],
        out_specs=[rows_of(block, n), whole(run, 2 * n), whole(before, run, 2 * n)],
        out_shape=[
            shape((run, n), BF16),
            shape((run, 2 * n), F32),
            shape((before, run, 2 * n), BF16),
        ],
        scratch_shapes=[pltpu.VMEM((before, run, 2 * n), F32)],
        compiler_params=params(),
        cost_estimate=cost(32 * run * (before * run + run) * n),
        name="attend_back",
    )(at, q, kv, prev, gatt, res, lse, tables)


def in_back_kernel(
    gq_ref, gkv_ref, got_ref, gup_ref, w_ref, table_ref, gin_ref, bias_ref, *y_refs
):
    n = gq_ref.shape[1]
    rows = y_refs[0].shape[0]
    half = len(y_refs) // 2
    sums = None
    for part in range(2):
        at = slice(part * half * rows, (part + 1) * half * rows)
        gkv = gkv_ref[at, :]
        for j in range(got_ref.shape[0]):
            gkv = gkv + got_ref[j, at, :].astype(F32)
        gkey = turn(gkv[:, :n], table_ref[:, at], back=True).astype(BF16)
        gin = jnp.concatenate(
            [gq_ref[at, :], gkey, gkv[:, n:].astype(BF16), gup_ref[at, :]], axis=1
        )
        gin_ref[at, :] = gin
        out = dot(gin, w_ref[...], NT).astype(BF16)
        for j in range(half):
            y_refs[part * half + j][...] = out[j * rows : (j + 1) * rows]
        term = jnp.sum(gin.astype(F32), 0, keepdims=True)
        sums = term if sums is None else sums + term
    bias_ref[...] = sums


def in_back(gq, gkv, got, gup, win, tables, rows):
    run = gq.shape[0]
    width, wide = win.shape
    shape = jax.ShapeDtypeStruct
    return pl.pallas_call(
        in_back_kernel,
        out_shape=[shape((run, wide), BF16), shape((1, wide), F32)]
        + [shape((rows, width), BF16)] * (run // rows),
        compiler_params=plain(),
        cost_estimate=cost(2 * run * width * wide, 2 * win.size),
        name="in_back",
    )(gq, gkv, got, gup, win, tables)


def weight_grad_kernel(count, slots, *refs):
    xs, ys, out_ref, hold_ref = refs[:count], refs[count:-2], refs[-2], refs[-1]

    @pl.when(pl.program_id(0) == 0)
    def _():
        col = 0
        for j in range(len(ys) // slots):
            for m in range(slots):
                y_ref = ys[j * slots + m]
                run, wide = y_ref.shape
                hold_ref[m * run : (m + 1) * run, col : col + wide] = y_ref[...]
            col += wide

    left = jnp.concatenate([ref[...] for ref in xs], axis=0)
    out_ref[...] = dot(left, hold_ref[...], TN).astype(BF16)


def weight_grad(xs, ys, block):
    rows, width = xs[0].shape
    tokens = rows * len(xs)
    slots = len(ys[0])
    wide = sum(part[0].shape[1] for part in ys)
    flat = [array for part in ys for array in part]
    return pl.pallas_call(
        functools.partial(weight_grad_kernel, len(xs), slots),
        grid=(width // block,),
        in_specs=[pl.BlockSpec((rows, block), lambda i: (0, i)) for _ in xs]
        + [whole(*array.shape) for array in flat],
        out_specs=rows_of(block, wide),
        out_shape=jax.ShapeDtypeStruct((width, wide), BF16),
        scratch_shapes=[pltpu.VMEM((tokens, wide), BF16)],
        compiler_params=params(),
        cost_estimate=cost(2 * tokens * width * wide, 2 * tokens * (width + wide)),
        name="weight_grad",
    )(*xs, *flat)


def at_part(index, size):
    return pl.ds(pl.multiple_of(index * size, size), size)


def pack_in_kernel(at_ref, qkv_ref, up_ref, *out_refs):
    count = len(out_refs)
    n, f = qkv_ref.shape[3] // count, up_ref.shape[2] // count
    for k, out_ref in enumerate(out_refs):
        place = (at_ref[0] + k) % count
        for j in range(3):
            out_ref[:, j * n : (j + 1) * n] = qkv_ref[0, j, :, at_part(place, n)]
        out_ref[:, 3 * n :] = up_ref[0, :, at_part(place, f)]


def pack_out_kernel(at_ref, out_w_ref, down_ref, *out_refs):
    count = len(out_refs)
    n, f = out_w_ref.shape[1] // count, down_ref.shape[1] // count
    for k, out_ref in enumerate(out_refs):
        place = (at_ref[0] + k) % count
        out_ref[:, :n] = out_w_ref[0, at_part(place, n), :].astype(F32).T.astype(BF16)
        out_ref[:, n:] = down_ref[0, at_part(place, f), :].astype(F32).T.astype(BF16)


def pack(kernel, at, first, second, layer, shape, count):
    def of_layer(array):
        rest = array.shape[1:]
        return pl.BlockSpec((1, *rest), lambda i: (layer,) + (0,) * len(rest))

    return pl.pallas_call(
        kernel,
        grid=(1,),
        in_specs=[pl.BlockSpec(memory_space=pltpu.SMEM), of_layer(first), of_layer(second)],
        out_specs=[whole(*shape)] * count,
        out_shape=[jax.ShapeDtypeStruct(shape, BF16)] * count,
        compiler_params=params(),
        cost_estimate=COST,
        name="pack",
    )(at, first, second)


def place_kernel(count, at_ref, *refs):
    blocks, out_ref, sems = refs[:count], refs[count], refs[count + 1]
    copies = [
        pltpu.make_async_copy(blocks[k], out_ref.at[at_ref[k]], sems.at[k]) for k in range(count)
    ]
    for copy in copies:
        copy.start()
    for copy in copies:
        copy.wait()


def place(places, blocks):
    count = len(blocks)
    return pl.pallas_call(
        functools.partial(place_kernel, count),
        in_specs=[pl.BlockSpec(memory_space=pltpu.SMEM)]
        + [pl.BlockSpec(memory_space=pltpu.VMEM)] * count,
        out_specs=pl.BlockSpec(memory_space=pl.ANY),
        out_shape=jax.ShapeDtypeStruct((count, *blocks[0].shape), BF16),
        scratch_shapes=[pltpu.SemaphoreType.DMA((count,))],
        compiler_params=plain(),
        cost_estimate=COST,
        name="place",
    )(jnp.stack(places), *blocks)


def unpack_in_kernel(held, at_ref, *refs):
    blocks, (qkv_ref, up_ref) = refs[: -2 - held], refs[-2:]
    count = len(blocks)
    n, f = qkv_ref.shape[3] // count, up_ref.shape[2] // count
    for k, block_ref in enumerate(blocks):
        source = (at_ref[0] + count - k) % count
        value = block_ref[...].astype(F32)
        for j in range(3):
            qkv_ref[0, j, :, at_part(source, n)] = value[:, j * n : (j + 1) * n]
        up_ref[0, :, at_part(source, f)] = value[:, 3 * n :]


def unpack_out_kernel(held, at_ref, *refs):
    blocks, (out_ref, down_ref) = refs[: -2 - held], refs[-2:]
    count = len(blocks)
    n, f = out_ref.shape[1] // count, down_ref.shape[1] // count
    for k, block_ref in enumerate(blocks):
        source = (at_ref[0] + count - k) % count
        value = block_ref[...].astype(F32)
        out_ref[0, at_part(source, n), :] = value[:, :n].T
        down_ref[0, at_part(source, f), :] = value[:, n:].T


def unpack(kernel, at, blocks, layer, shapes, held):
    def of_layer(shape):
        return pl.BlockSpec((1, *shape[1:]), lambda i: (layer,) + (0,) * (len(shape) - 1))

    held = held or []
    first = 1 + len(blocks)
    return pl.pallas_call(
        functools.partial(kernel, len(held)),
        grid=(1,),
        in_specs=[pl.BlockSpec(memory_space=pltpu.SMEM)]
        + [whole(*block.shape) for block in blocks]
        + [pl.BlockSpec(memory_space=pl.ANY) for _ in held],
        out_specs=[of_layer(shape) for shape in shapes],
        out_shape=[jax.ShapeDtypeStruct(shape, F32) for shape in shapes],
        input_output_aliases={first + j: j for j in range(len(held))},
        compiler_params=params(),
        cost_estimate=COST,
        name="unpack",
    )(at, *blocks, *held)


def norm_kernel(count, *refs):
    parts = refs[:count]
    hidden_ref, bias_ref, gain_ref, shift_ref, next_ref, normed_ref = refs[count:]
    hidden = hidden_ref[...] + bias_ref[...]
    for ref in parts:
        hidden = hidden + ref[...].astype(F32)
    next_ref[...] = hidden
    normed_ref[...] = layer_norm(hidden, gain_ref[...], shift_ref[...]).astype(BF16)


def sum_norm(parts, hidden, bias, gain, shift):
    shape = jax.ShapeDtypeStruct
    return pl.pallas_call(
        functools.partial(norm_kernel, len(parts)),
        out_shape=[shape(hidden.shape, F32), shape(hidden.shape, BF16)],
        compiler_params=plain(),
        cost_estimate=COST,
        name="sum_norm",
    )(*parts, hidden, bias[None], gain[None], shift[None])


def norm_back_kernel(count, *refs):
    parts = refs[:count]
    hidden_ref, grad_ref, gain_ref, next_ref, low_ref, ggain_ref, gshift_ref = refs[count:]
    total = parts[0][...].astype(F32)
    for ref in parts[1:]:
        total = total + ref[...].astype(F32)
    hidden = hidden_ref[...]
    centred = hidden - jnp.mean(hidden, -1, keepdims=True)
    factor = lax.rsqrt(jnp.mean(centred * centred, -1, keepdims=True) + 1e-05)
    xhat = centred * factor
    ggain_ref[...] = jnp.sum(total * xhat, 0, keepdims=True)
    gshift_ref[...] = jnp.sum(total, 0, keepdims=True)
    inner = total * gain_ref[...]
    first = jnp.mean(inner, -1, keepdims=True)
    second = jnp.mean(inner * xhat, -1, keepdims=True)
    grad = grad_ref[...] + factor * (inner - first - xhat * second)
    next_ref[...] = grad
    low_ref[...] = grad.astype(BF16)


def sum_norm_back(parts, hidden, grad, gain):
    shape = jax.ShapeDtypeStruct
    row = shape((1, hidden.shape[1]), F32)
    return pl.pallas_call(
        functools.partial(norm_back_kernel, len(parts)),
        out_shape=[shape(hidden.shape, F32), shape(hidden.shape, BF16), row, row],
        compiler_params=plain(),
        cost_estimate=COST,
        name="sum_norm_back",
    )(*parts, hidden, grad, gain[None])


class Stages:
    def __init__(self, token):
        self.token = token
        self.active = []
        self.count = 0

    def spawn(self, process):
        self.active.append((process, None))

    def hold(self, *arrays):
        return lax.optimization_barrier((self.token, *arrays))[1:]

    def step(self):
        self.count += 1
        given, moved = [], True
        while moved:
            moved, todo, self.active = False, self.active, []
            for process, value in todo:
                try:
                    out = process.send(value)
                except StopIteration:
                    moved = True
                    continue
                if out is WAIT:
                    self.active.append((process, None))
                else:
                    moved = True
                    given.append((process, out))
        flat, tree = jax.tree.flatten([out for _, out in given])
        flat = lax.optimization_barrier((self.token, *flat))
        self.token = flat[0]
        outs = jax.tree.unflatten(tree, flat[1:])
        self.active += [(process, out) for (process, _), out in zip(given, outs)]

    def run(self):
        while self.active:
            before = [id(process) for process, _ in self.active]
            self.step()
            assert self.count < 500


WAIT = object()


def until(ready):
    while not ready():
        yield WAIT


class Group:
    def __init__(self):
        self.S = lax.axis_size("slot")
        self.C = lax.axis_size("ctx")
        self.T = lax.axis_size("tp")
        self.s = lax.axis_index("slot")
        self.c = lax.axis_index("ctx")
        self.t = lax.axis_index("tp")
        assert self.S == 4 and self.T == 4
        self.far, self.near = self.T // 2, 1
        self.corner = (self.t % 2) * 2 + self.t // 2
        self.slot_at = self.s.astype(jnp.int32)[None]

    def swap(self, block, bit):
        return lax.ppermute(block, "tp", [(i, i ^ bit) for i in range(self.T)])

    def shift(self, block, k):
        S = self.S
        return lax.ppermute(block, "slot", [(i, (i + k) % S) for i in range(S)])

    def parts_of(self, array, rows):
        return [
            lax.dynamic_slice_in_dim(array, (self.corner ^ b) * rows, rows, 0)
            for b in range(self.T)
        ]

    def in_order(self, parts):
        rows = parts[0].shape[0]
        array = jnp.zeros((self.T * rows, *parts[0].shape[1:]), parts[0].dtype)
        for b, part in enumerate(parts):
            array = lax.dynamic_update_slice_in_dim(array, part, (self.corner ^ b) * rows, 0)
        return array

    def gather(self, block, own_parts, ready, sent=lambda: None):
        blocks = {0: block}
        if own_parts is not None:
            ready(0, own_parts)
        waiting = []
        order = [0, 1, 3, 2]
        for r in range(6):
            for k, parts in waiting:
                ready(k, parts + [self.swap(parts[1], self.near)])
            waiting = []
            if r == 5:
                return
            fresh = {}
            if r == 0:
                fresh[1] = self.shift(block, -1)
            elif r == 1:
                fresh[3] = self.shift(block, 1)
            elif r == 2:
                fresh["down"] = lax.ppermute(blocks[1], "slot", [(1, 0), (2, 1)])
                fresh["up"] = lax.ppermute(blocks[3], "slot", [(1, 2), (2, 3)])
            if r == 3:
                blocks[2] = lax.optimization_barrier(
                    jnp.where(self.s < 2, blocks["down"], blocks["up"])
                )
            if r < 4 and (r > 0 or own_parts is None):
                k = order[r]
                mine = blocks[k]
                parts = [mine, self.swap(mine, self.far), self.swap(mine, self.near)]
                fresh, parts = yield fresh, parts
                waiting = [(k, parts)]
            elif r < 4:
                (fresh,) = yield (fresh,)
            blocks.update(fresh)
            if r == 2:
                sent()

    def scatter(self, make, there, finish):
        order = [2, 1, 3, 0]
        near, far, from_two = {}, {}, {}
        got = []

        def total(k, *more):
            return lax.optimization_barrier(
                sum((a.astype(F32) for a in more), sum(a.astype(F32) for a in far[k])).astype(BF16)
            )

        for r in range(5):
            if r < 4:
                yield from until(lambda: there(order[r]))
            sent = {}
            if r >= 1:
                keep, give = near[order[r - 1]]
                away = (keep[1].astype(F32) + give[1].astype(F32)).astype(BF16)
                sent["far"] = (keep[0], give[0], self.swap(away, self.far))
            if r == 2:
                two = total(2)
                sent["up"] = lax.ppermute(two, "slot", [(0, 1), (1, 2)])
                sent["down"] = lax.ppermute(two, "slot", [(2, 1), (3, 2)])
            if r == 3:
                sent["got"] = self.shift(total(1, from_two["up"]), 1)
            if r == 4:
                sent["got"] = self.shift(total(3, from_two["down"]), -1)
            if r < 4:
                keep0, keep1, give0, give1 = make(order[r])
                sent["near"] = (
                    (keep0, keep1),
                    (self.swap(give0, self.near), self.swap(give1, self.near)),
                )
            sent, got = yield sent, got
            if "near" in sent:
                near[order[r]] = sent["near"]
            if "far" in sent:
                far[order[r - 1]] = sent["far"]
            if "up" in sent:
                from_two = sent
            if "got" in sent:
                got = got + [sent["got"]]
        finish(list(far[0]) + got)

    def ctx_before(self, block):
        C = self.C
        got = [
            lax.ppermute(block, "ctx", [(i, i + j) for i in range(C - j)])[None]
            for j in range(1, C)
        ]
        return got[0] if C == 2 else jnp.concatenate(got)

    def ctx_return(self, blocks):
        C = self.C
        got = [
            lax.ppermute(blocks[j - 1], "ctx", [(i, i - j) for i in range(j, C)])[None]
            for j in range(1, C)
        ]
        return got[0] if C == 2 else jnp.concatenate(got)

    def ctx_others(self, block):
        C = self.C
        return [
            lax.ppermute(block, "ctx", [(i, (i + j) % C) for i in range(C)]) for j in range(1, C)
        ]

    def gather_weights(self, pieces, done, sent):
        S, C = self.S, self.C
        d, wide = pieces[0].shape
        blocks, places = [pieces[0]], [0]
        others = []
        for shifts, back in (([1, 3], [0]), ([2], [1, 3]), ([], [2])):
            ready = dict(zip(places, blocks))
            got = [self.shift(pieces[k], k) for k in shifts]
            new = [self.ctx_others(ready[k]) for k in back]
            got, new, blocks, others, pieces = yield got, new, blocks, others, pieces
            blocks, places = blocks + got, places + shifts
            others = others + list(zip(back, new))
            if shifts == [2]:
                sent()
        flat, at = [], []
        for k, block in zip(places, blocks):
            flat.append(block)
            at.append(self.c * S + (self.s - k) % S)
        for k, found in others:
            for j, block in enumerate(found):
                flat.append(block)
                at.append((self.c - j - 1) % C * S + (self.s - k) % S)
        done(place(at, flat).reshape(C * S * d, wide))

    def gather_weights_later(self, pieces, done, sent, steps):
        S, C = self.S, self.C
        d, wide = pieces[0].shape
        first, pieces = yield [self.shift(pieces[1], 1)], pieces
        more, first, pieces = yield [self.shift(pieces[3], 3)], first, pieces
        first = first + more
        second, first, pieces = yield [self.shift(pieces[2], 2)], first, pieces
        sent()
        flat = place(
            [(self.s - k) % S for k in (0, 1, 3, 2)], [pieces[0], first[0], first[1], second[0]]
        )
        array = lax.all_gather(flat, "ctx")
        for _ in range(steps):
            yield ()
        done(array.reshape(C * S * d, wide))

    def scatter_weights(self, grad, done, steps):
        S, C = self.S, self.C
        wide = grad.shape[1]
        d = grad.shape[0] // (S * C)
        own = lax.psum_scatter(grad.reshape(C, S, d, wide), "ctx")
        for _ in range(steps):
            yield ()
        pieces = [
            lax.dynamic_index_in_dim(own, (self.s + k) % S, 0, keepdims=False) for k in range(S)
        ]
        first, pieces = yield [self.shift(pieces[1], 1)], pieces
        more, first, pieces = yield [self.shift(pieces[3], 3)], first, pieces
        first = first + more
        second, first, pieces = yield [self.shift(pieces[2], 2)], first, pieces
        done([pieces[0], first[0], second[0], first[1]])

    def add_up(self, small, part, finish):
        cut = small.shape[0]
        both = jnp.concatenate([small, part])
        for axis, size in (("slot", self.S), ("ctx", self.C)):
            bit = 1
            while bit < size:
                got = lax.ppermute(both, axis, [(i, i ^ bit) for i in range(size)])
                got, both = yield got, both
                both = both + got
                bit *= 2
        small, part = both[:cut], both[cut:]
        for bit in (self.far, self.near):
            got = self.swap(small, bit)
            got, small, part = yield got, small, part
            small = small + got
        finish(small, part)


def on_device(
    inputs,
    lengths,
    ln_gain,
    ln_shift,
    w_qkv,
    b_qkv,
    w_out,
    b_out,
    w_up,
    b_up,
    w_down,
    b_down,
    cotangent,
):
    grp = Group()
    S, C, T = grp.S, grp.C, grp.T
    _, run, width = inputs.shape
    rows = run // T
    nt, ft = w_qkv.shape[3], w_up.shape[2]
    n, f = nt // S, ft // S
    d = w_up.shape[1]
    block = run // 2
    stages = Stages(lengths)

    def to_held(array):
        lead = array.shape[:-1]
        return array.reshape(*lead, S, C, d).swapaxes(-3, -2).reshape(*lead, width)

    def from_held(array):
        lead = array.shape[:-1]
        return array.reshape(*lead, C, S, d).swapaxes(-3, -2).reshape(*lead, width)

    inputs, cotangent = to_held(inputs), to_held(cotangent)
    ln_gain, ln_shift = to_held(ln_gain), to_held(ln_shift)
    b_out, b_down = to_held(b_out), to_held(b_down)
    local = jnp.arange(run, dtype=jnp.int32)
    positions = grp.c * run + (local // rows ^ grp.corner) * rows + local % rows
    tables = rotary_tables(positions, n // HD)
    valid = (positions < lengths[0]).astype(F32)[:, None]
    own_valid = valid[:rows]
    box = {}
    kept = [[None] * S for _ in range(LAYERS)]
    normed = [[None] * S for _ in range(LAYERS)]
    grad_branch = [[None] * S for _ in range(LAYERS)]
    middle = [[None] * S for _ in range(LAYERS)]
    gins = [[None] * S for _ in range(LAYERS)]
    bias_sums = [[None] * S for _ in range(LAYERS)]
    small_sums = [None] * LAYERS

    def bias_part(bias, size):
        return lax.dynamic_slice_in_dim(bias, grp.s * size, size, bias.ndim - 1)

    biases = [
        jnp.concatenate([bias_part(b_qkv[layer], n).reshape(-1), bias_part(b_up[layer], f)])[None]
        for layer in range(LAYERS)
    ]
    def after(*keys):
        return until(lambda: all(key in box for key in keys))

    def mark(*key):
        return lambda *value: box.__setitem__(key, value[0] if value else True)

    def lengths_of_all():
        got = yield [grp.shift(lengths, -k) for k in range(1, S)]
        for k, value in enumerate([lengths] + list(got)):
            box["at", k] = jnp.concatenate([value, grp.c[None], grp.corner[None]])

    def in_weights(layer, *keys, later=None):
        yield from after(*keys)
        pieces = pack(
            pack_in_kernel, grp.slot_at, w_qkv, w_up, layer, (d, 3 * n + f), S
        )
        pieces = list(stages.hold(*pieces))
        if later is None:
            yield from grp.gather_weights(pieces, mark("win", layer), mark("win sent", layer))
        else:
            yield from grp.gather_weights_later(
                pieces, mark("win", layer), mark("win sent", layer), later
            )

    def out_weights(layer, *keys, later=None):
        yield from after(*keys)
        pieces = pack(pack_out_kernel, grp.slot_at, w_out, w_down, layer, (d, n + f), S)
        pieces = list(stages.hold(*pieces))
        if later is None:
            yield from grp.gather_weights(pieces, mark("wout", layer), mark("wout sent", layer))
        else:
            yield from grp.gather_weights_later(
                pieces, mark("wout", layer), mark("wout sent", layer), later
            )

    def forward_slot(layer, k, parts):
        yield from after(("win", layer), ("at", k))
        normed[layer][k] = parts
        q, kv, up, act = in_project(parts, box["win", layer], biases[layer], tables, n)
        if k == 2:
            prev = grp.ctx_before(kv)
            q, kv, up, act = yield q, kv, up, act
        else:
            q, kv, up, act = yield q, kv, up, act
            q, kv, up, act, prev = yield q, kv, up, act, grp.ctx_before(kv)
        res, att, lse = attend(box["at", k], q, kv, prev, block, rows)
        box["attended", layer, k] = True
        kept[layer][k] = (q, kv, prev, up, act, res, att, lse)

    def make_forward(layer):
        def make(k):
            return out_project(kept[layer][k][6], kept[layer][k][4], box["wout", layer], rows)

        return make

    def there_forward(layer):
        return lambda k: ("attended", layer, k) in box and ("wout", layer) in box

    def backward_slot(layer, k, parts):
        yield from after(("wout", layer), ("attended", layer, k))
        grad_branch[layer][k] = parts
        if all(grad_branch[layer]):
            box["grad gathered", layer] = True
        q, kv, prev, up, _, res, _, lse = kept[layer][k]
        gatt, gup = out_back(parts, box["wout", layer], up, n)
        gq, gkv, gprev = attend_back(
            box["at", k], q, kv, prev, gatt, res, lse, tables, block, rows
        )
        if k == 2:
            got = grp.ctx_return(gprev)
            gq, gkv, gup = yield gq, gkv, gup
        else:
            gq, gkv, gup, gprev = yield gq, gkv, gup, gprev
            gq, gkv, gup, got = yield gq, gkv, gup, grp.ctx_return(gprev)
        middle[layer][k] = (gq, gkv, got, gup)
        box["middle", layer, k] = True

    def make_backward(layer):
        def make(k):
            gq, gkv, got, gup = middle[layer][k]
            gin, bias_sum, *parts = in_back(gq, gkv, got, gup, box["win", layer], tables, rows)
            gins[layer][k] = gin
            bias_sums[layer][k] = bias_sum[0]
            box["gin", layer, k] = True
            return parts

        return make

    def there_backward(layer):
        return lambda k: ("middle", layer, k) in box

    def slot_ready(kind, layer):
        return lambda m, parts: stages.spawn(kind(layer, m, parts))

    def out_grads(layer, *keys, steps=4):
        yield from after(*keys)
        grad = weight_grad(
            [part for parts in grad_branch[layer] for part in parts],
            [[kept[layer][k][6] for k in range(S)], [kept[layer][k][4] for k in range(S)]],
            block,
        )
        (grad,) = yield (grad,)
        yield from grp.scatter_weights(grad, mark("grad out", layer), steps)

    def in_grads(layer, *keys, steps=4):
        yield from after(*keys, *[("gin", layer, k) for k in range(S)])
        grad = weight_grad(
            [part for parts in normed[layer] for part in parts], [gins[layer]], block
        )
        (grad,) = yield (grad,)
        yield from grp.scatter_weights(grad, mark("grad in", layer), steps)

    def first_gather(*keys):
        yield from after(*keys)
        own_rows = grp.parts_of(inputs[0], rows)
        parts = [
            layer_norm(part.astype(F32), ln_gain[0], ln_shift[0]).astype(BF16) for part in own_rows
        ]
        box["hidden", 0] = own_rows[0].astype(F32)
        parts = list(stages.hold(*parts))
        yield from grp.gather(
            parts[0], parts, slot_ready(forward_slot, 0), mark("normed sent", 0)
        )

    def next_gather(layer):
        yield from after(("hidden", layer))
        yield from grp.gather(
            box["normed", layer], None, slot_ready(forward_slot, layer), mark("normed sent", layer)
        )

    def forward_sum(layer, *keys):
        yield from after(*keys)

        def finish(parts):
            later = min(layer + 1, LAYERS - 1)
            box["hidden", layer + 1], box["normed", layer + 1] = sum_norm(
                parts,
                box["hidden", layer],
                b_out[layer] + b_down[layer],
                ln_gain[later],
                ln_shift[later],
            )

        yield from grp.scatter(make_forward(layer), there_forward(layer), finish)

    def last_gradient(*keys):
        yield from after(*keys)
        parts = [
            part.astype(F32) * valid[b * rows : (b + 1) * rows]
            for b, part in enumerate(grp.parts_of(cotangent[0], rows))
        ]
        box["grad", LAYERS] = parts[0]
        parts = list(stages.hold(*[part.astype(BF16) for part in parts]))
        yield from grp.gather(
            parts[0], parts, slot_ready(backward_slot, LAYERS - 1), mark("grad sent", LAYERS)
        )

    def next_gradient(layer):
        yield from after(("grad", layer))
        yield from grp.gather(
            box["grad low", layer],
            None,
            slot_ready(backward_slot, layer - 1),
            mark("grad sent", layer),
        )

    def backward_sum(layer):
        def finish(parts):
            grad_bias_out = jnp.sum(box["grad", layer + 1], 0)
            box["grad", layer], box["grad low", layer], grad_gain, grad_shift = sum_norm_back(
                parts, box["hidden", layer], box["grad", layer + 1], ln_gain[layer]
            )
            small_sums[layer] = (grad_gain[0], grad_shift[0], grad_bias_out)

        yield from grp.scatter(make_backward(layer), there_backward(layer), finish)

    def all_sums(*keys):
        yield from after(*keys)
        spread = []
        for layer in range(LAYERS):
            total = sum(bias_sums[layer][1:], bias_sums[layer][0])
            pieces = jnp.zeros((3 * nt + ft,), F32)
            for i in range(3):
                pieces = lax.dynamic_update_slice_in_dim(
                    pieces, total[i * n : (i + 1) * n], i * nt + grp.s * n, 0
                )
            spread.append(
                lax.dynamic_update_slice_in_dim(pieces, total[3 * n :], 3 * nt + grp.s * f, 0)
            )
        yield from grp.add_up(
            jnp.concatenate([piece for entry in small_sums for piece in entry]),
            jnp.concatenate(spread),
            lambda small, part: box.__setitem__("sums", (small, part)),
        )

    def all_rows(key, value, name):
        yield from after(key)
        block = from_held(value())
        parts = [block, grp.swap(block, grp.far), grp.swap(block, grp.near)]
        parts = yield parts
        box[name] = grp.in_order(list(parts) + [grp.swap(parts[1], grp.near)])[None]

    def all_grads(layer, *keys):
        yield from after(("grad in", layer), ("grad out", layer), *keys)
        box["final in", layer] = unpack(
            unpack_in_kernel,
            grp.slot_at,
            box["grad in", layer],
            layer,
            ((LAYERS, 3, d, nt), (LAYERS, d, ft)),
            box.get(("final in", layer + 1)),
        )
        box["final out", layer] = unpack(
            unpack_out_kernel,
            grp.slot_at,
            box["grad out", layer],
            layer,
            ((LAYERS, nt, d), (LAYERS, ft, d)),
            box.get(("final out", layer + 1)),
        )

    last = LAYERS - 1
    stages.spawn(in_weights(0))
    stages.spawn(lengths_of_all())
    stages.spawn(first_gather(("win sent", 0)))
    stages.spawn(forward_sum(0))
    stages.spawn(out_weights(0, ("normed sent", 0)))
    for layer in range(1, LAYERS):
        stages.spawn(in_weights(layer, ("wout", layer - 1), later=3))
        stages.spawn(next_gather(layer))
        if layer < last:
            stages.spawn(forward_sum(layer))
        stages.spawn(out_weights(layer, ("win sent", layer), later=3))
    stages.spawn(last_gradient(("normed sent", last)))
    for layer in reversed(range(LAYERS)):
        stages.spawn(backward_sum(layer))
        if layer > 0:
            stages.spawn(next_gradient(layer))
    stages.spawn(forward_sum(last, ("grad sent", last)))
    for layer in reversed(range(LAYERS)):
        stages.spawn(out_grads(layer, ("grad gathered", layer)))
        stages.spawn(in_grads(layer))
        stages.spawn(all_grads(layer, *([] if layer == last else [("final in", layer + 1)])))
    stages.spawn(
        all_rows(
            ("hidden", LAYERS), lambda: (box["hidden", LAYERS] * own_valid).astype(BF16), "block out"
        )
    )
    stages.spawn(all_rows(("grad", 0), lambda: box["grad low", 0], "grad input"))
    stages.spawn(all_sums(("grad", 0)))
    stages.run()

    small, part = box["sums"]
    small = from_held(small.reshape(LAYERS, 3, width))
    part = part.reshape(LAYERS, 3 * nt + ft)
    grad_qkv, grad_up = box["final in", 0]
    grad_out, grad_down = box["final out", 0]
    return (
        box["block out"],
        box["grad input"],
        small[:, 0],
        small[:, 1],
        grad_qkv,
        part[:, : 3 * nt].reshape(LAYERS, 3, nt),
        grad_out,
        small[:, 2],
        grad_up,
        part[:, 3 * nt :],
        grad_down,
        small[:, 2],
    )


def solution(mesh):
    return jax.shard_map(
        on_device,
        mesh=mesh,
        in_specs=(
            P("slot", "ctx", None),
            P("slot"),
            P(),
            P(),
            P(None, None, ("slot", "ctx"), "tp"),
            P(None, None, "tp"),
            P(None, "tp", ("slot", "ctx")),
            P(),
            P(None, ("slot", "ctx"), "tp"),
            P(None, "tp"),
            P(None, "tp", ("slot", "ctx")),
            P(),
            P("slot", "ctx", None),
        ),
        out_specs=(
            P("slot", "ctx", None),
            P("slot", "ctx", None),
            P(),
            P(),
            P(None, None, ("slot", "ctx"), "tp"),
            P(None, None, "tp"),
            P(None, "tp", ("slot", "ctx")),
            P(),
            P(None, ("slot", "ctx"), "tp"),
            P(None, "tp"),
            P(None, "tp", ("slot", "ctx")),
            P(),
        ),
        check_vma=False,
    )
```

```python
import functools
import math

import jax
import jax.numpy as jnp
from jax import lax
from jax.experimental import pallas as pl
from jax.experimental.pallas import tpu as pltpu
from jax.sharding import PartitionSpec as P

HD = 64
ROT = 32
LAYERS = 2

masked = -1e30
F32 = jnp.float32
BF16 = jnp.bfloat16
NT = (((1,), (1,)), ((), ()))
TN = (((0,), (0,)), ((), ()))
VMEM_LIMIT = 20 * 1024 * 1024


def dot(a, b, dims=None):
    if dims is None:
        return jnp.dot(a, b, preferred_element_type=F32)
    return lax.dot_general(a, b, dims, preferred_element_type=F32)


def gelu_tanh(value):
    inner = 0.7978845608028654 * (value + 0.044715 * value * value * value)
    return 0.5 * value * (1.0 + jnp.tanh(inner))


def gelu_slope(value):
    square = value * value
    inner = 0.7978845608028654 * (value + 0.044715 * value * square)
    bend = jnp.tanh(inner)
    slope = 0.7978845608028654 * (1.0 + 3.0 * 0.044715 * square)
    return 0.5 * (1.0 + bend) + 0.5 * value * (1.0 - bend * bend) * slope


def layer_norm(hidden, gain, shift):
    centre = jnp.mean(hidden, -1, keepdims=True)
    centred = hidden - centre
    variance = jnp.mean(centred * centred, -1, keepdims=True)
    return centred * lax.rsqrt(variance + 1e-05) * gain + shift


def rotary_tables(positions, heads):
    half_rot = ROT // 2
    freqs = jnp.exp(jnp.arange(half_rot, dtype=F32) * (-2.0 * math.log(10000.0) / ROT))
    angles = positions.astype(F32)[:, None] * freqs[None, :]
    cosine, sine = jnp.cos(angles), jnp.sin(angles)
    rows = positions.shape[0]
    rest = jnp.zeros((rows, HD - ROT), F32)
    none = jnp.zeros_like(sine)
    same = jnp.concatenate([cosine, cosine, rest + 1.0], axis=1)
    ahead = jnp.concatenate([-sine, none, rest], axis=1)
    behind = jnp.concatenate([none, sine, rest], axis=1)
    return jnp.stack([jnp.tile(part, (1, heads)) for part in (same, ahead, behind)])


def turn(value, tables, back=False):
    width = value.shape[1]
    half_rot = ROT // 2
    moved = (
        pltpu.roll(value, width - half_rot, 1) * tables[1] + pltpu.roll(value, half_rot, 1) * tables[2]
    )
    stay = value * tables[0]
    return stay - moved if back else stay + moved


def in_kernel(count, *refs):
    xs = refs[:count]
    w_ref, bias_ref, table_ref, q_ref, kv_ref, up_ref, act_ref = refs[count:]
    n = q_ref.shape[1]
    rows = xs[0].shape[0]
    half = count // 2
    for part in range(2):
        at = slice(part * half * rows, (part + 1) * half * rows)
        x = jnp.concatenate([ref[...] for ref in xs[part * half : (part + 1) * half]], axis=0)
        out = dot(x, w_ref[...]) + bias_ref[...]
        tables = table_ref[:, at]
        q_ref[at, :] = turn(out[:, :n], tables).astype(BF16)
        kv_ref[at, :n] = turn(out[:, n : 2 * n], tables).astype(BF16)
        kv_ref[at, n:] = out[:, 2 * n : 3 * n].astype(BF16)
        up = out[:, 3 * n :]
        up_ref[at, :] = up
        act_ref[at, :] = gelu_tanh(up).astype(BF16)


def rows_of(block, width):
    return pl.BlockSpec((block, width), lambda i: (i, 0))


def whole(*shape):
    return pl.BlockSpec(shape, lambda i: (0,) * len(shape))


def params():
    return pltpu.CompilerParams(
        dimension_semantics=("arbitrary",), vmem_limit_bytes=VMEM_LIMIT
    )


def plain():
    return pltpu.CompilerParams(vmem_limit_bytes=VMEM_LIMIT)


def cost(flops, moved=0):
    return pl.CostEstimate(
        flops=int(COST_SCALE * flops), bytes_accessed=int(moved), transcendentals=0
    )


COST_SCALE = 1.5
COST = cost(1000)


def in_project(xs, win, bias, tables, n):
    rows, width = xs[0].shape
    run = rows * len(xs)
    f = win.shape[1] - 3 * n
    shape = jax.ShapeDtypeStruct
    return pl.pallas_call(
        functools.partial(in_kernel, len(xs)),
        out_shape=[
            shape((run, n), BF16),
            shape((run, 2 * n), BF16),
            shape((run, f), F32),
            shape((run, f), BF16),
        ],
        compiler_params=plain(),
        cost_estimate=cost(2 * run * width * win.shape[1], 2 * win.size),
        name="in_project",
    )(*xs, win, bias, tables)


def diagonal(block, corner, rows_each, room):
    key = lax.broadcasted_iota(jnp.int32, (block, block), 0)
    query = lax.broadcasted_iota(jnp.int32, (1, block), 1)
    inside = corner % (block // rows_each)

    def at(row):
        return (row // rows_each ^ inside) * rows_each + row % rows_each

    return at(key) < jnp.minimum(at(query) + 1, room)


def attend_kernel(rows_each, at_ref, q_ref, own_ref, prev_ref, res_ref, att_ref, lse_ref):
    length, place, corner = at_ref[0], at_ref[1], at_ref[2]
    block, n = q_ref.shape
    heads = n // HD
    run = own_ref.shape[0]
    i = pl.program_id(0)
    flip = corner * rows_each // block
    home = i ^ flip
    first = place * run + home * block

    @pl.when(first >= length)
    def _():
        res_ref[...] = jnp.zeros_like(res_ref)
        att_ref[...] = jnp.zeros_like(att_ref)
        lse_ref[...] = jnp.zeros_like(lse_ref)

    @pl.when(first < length)
    def _():
        lane = lax.broadcasted_iota(jnp.int32, (1, n), 1)
        q = q_ref[...].astype(F32) * HD ** (-0.5)
        qs = [jnp.where(lane // HD == h, q, 0.0).astype(BF16) for h in range(heads)]

        def step(keys, values, carry, limit=None):
            out = []
            for h in range(heads):
                top, total, accum = carry[h]
                scores = dot(keys, qs[h], NT)
                if limit is not None:
                    scores = jnp.where(limit, scores, masked)
                new_top = jnp.maximum(top, jnp.max(scores, 0, keepdims=True))
                probs = jnp.exp(scores - new_top)
                shrink = jnp.exp(top - new_top)
                total = total * shrink + jnp.sum(probs, 0, keepdims=True)
                accum = accum * shrink + dot(values, probs.astype(BF16), TN)
                out.append((new_top, total, accum))
            return tuple(out)

        carry = tuple(
            (
                jnp.full((1, block), masked, F32),
                jnp.zeros((1, block), F32),
                jnp.zeros((n, block), F32),
            )
            for _ in range(heads)
        )
        inner = run // block

        def prev_step(j, carry):
            rows = pl.ds(pl.multiple_of((j % inner) * block, block), block)
            return step(prev_ref[j // inner, rows, :n], prev_ref[j // inner, rows, n:], carry)

        carry = lax.fori_loop(0, place * inner, prev_step, carry)

        def own_step(j, carry):
            rows = pl.ds(pl.multiple_of((j ^ flip) * block, block), block)
            return step(own_ref[rows, :n], own_ref[rows, n:], carry)

        carry = lax.fori_loop(0, home, own_step, carry)
        limit = diagonal(block, corner, rows_each, length - first)
        rows = pl.ds(pl.multiple_of(i * block, block), block)
        carry = step(own_ref[rows, :n], own_ref[rows, n:], carry, limit)
        parts = []
        for h in range(heads):
            top, total, accum = carry[h]
            lse_ref[h : h + 1, :] = top + jnp.log(total)
            parts.append(accum[h * HD : (h + 1) * HD] / total)
        result = jnp.concatenate(parts, axis=0).T
        res_ref[...] = result
        att_ref[...] = result.astype(BF16)


def attend(at, q, kv, prev, block, rows_each):
    run, n = q.shape
    heads = n // HD
    before = prev.shape[0]
    shape = jax.ShapeDtypeStruct
    tiles = run * (before * run + run)
    return pl.pallas_call(
        functools.partial(attend_kernel, rows_each),
        grid=(run // block,),
        in_specs=[
            pl.BlockSpec(memory_space=pltpu.SMEM),
            rows_of(block, n),
            whole(run, 2 * n),
            whole(before, run, 2 * n),
        ],
        out_specs=[
            rows_of(block, n),
            rows_of(block, n),
            pl.BlockSpec((heads, block), lambda i: (0, i)),
        ],
        out_shape=[shape((run, n), F32), shape((run, n), BF16), shape((heads, run), F32)],
        compiler_params=params(),
        cost_estimate=cost(32 * run * (before * run + run) * n),
        name="attend",
    )(at, q, kv, prev)


def out_kernel(att_ref, act_ref, w_ref, *y_refs):
    rows = y_refs[0].shape[0]
    half = len(y_refs) // 2
    for part in range(2):
        at = slice(part * half * rows, (part + 1) * half * rows)
        both = jnp.concatenate([att_ref[at, :], act_ref[at, :]], axis=1)
        out = dot(both, w_ref[...], NT).astype(BF16)
        for j in range(half):
            y_refs[part * half + j][...] = out[j * rows : (j + 1) * rows]


def out_project(att, act, wout, rows):
    count = att.shape[0] // rows
    return pl.pallas_call(
        out_kernel,
        out_shape=[jax.ShapeDtypeStruct((rows, wout.shape[0]), BF16)] * count,
        compiler_params=plain(),
        cost_estimate=cost(2 * att.shape[0] * wout.size, 2 * wout.size),
        name="out_project",
    )(att, act, wout)


def out_back_kernel(count, *refs):
    xs = refs[:count]
    w_ref, up_ref, gatt_ref, gup_ref = refs[count:]
    n = gatt_ref.shape[1]
    rows = xs[0].shape[0]
    half = count // 2
    for part in range(2):
        at = slice(part * half * rows, (part + 1) * half * rows)
        x = jnp.concatenate([ref[...] for ref in xs[part * half : (part + 1) * half]], axis=0)
        out = dot(x, w_ref[...])
        gatt_ref[at, :] = out[:, :n].astype(BF16)
        gup_ref[at, :] = (out[:, n:] * gelu_slope(up_ref[at, :])).astype(BF16)


def out_back(xs, wout, up, n):
    run, f = up.shape
    shape = jax.ShapeDtypeStruct
    return pl.pallas_call(
        functools.partial(out_back_kernel, len(xs)),
        out_shape=[shape((run, n), BF16), shape((run, f), BF16)],
        compiler_params=plain(),
        cost_estimate=cost(2 * run * wout.size, 2 * wout.size),
        name="out_back",
    )(*xs, wout, up)


def attend_back_kernel(
    rows_each, at_ref, q_ref, own_ref, prev_ref, gatt_ref, res_ref, lse_ref, table_ref,
    gq_ref, gown_ref, gprev_ref, hold_ref,
):
    length, place, corner = at_ref[0], at_ref[1], at_ref[2]
    block, n = q_ref.shape
    heads = n // HD
    run = own_ref.shape[0]
    before = prev_ref.shape[0]
    i = pl.program_id(0)
    flip = corner * rows_each // block
    home = i ^ flip
    first = place * run + home * block

    @pl.when(i == 0)
    def _():
        gown_ref[...] = jnp.zeros_like(gown_ref)
        hold_ref[...] = jnp.zeros_like(hold_ref)

    @pl.when(first >= length)
    def _():
        gq_ref[...] = jnp.zeros_like(gq_ref)

    @pl.when(first < length)
    def _():
        lane = lax.broadcasted_iota(jnp.int32, (1, n), 1)
        q, gatt = q_ref[...], gatt_ref[...]
        pick = [lane // HD == h for h in range(heads)]
        zero = jnp.zeros((), BF16)
        qs = [jnp.where(p, q, zero) for p in pick]
        gs = [jnp.where(p, gatt, zero) for p in pick]
        shared = (gatt.astype(F32) * res_ref[...]).T
        deltas = [jnp.sum(shared[h * HD : (h + 1) * HD], 0, keepdims=True) for h in range(heads)]
        sums = [lse_ref[h : h + 1, :] for h in range(heads)]
        scale = HD ** (-0.5)

        def step(keys, values, carry, limit=None):
            gkeys = gvalues = None
            out = []
            for h in range(heads):
                scores = dot(keys, qs[h], NT) * scale
                if limit is not None:
                    scores = jnp.where(limit, scores, masked)
                probs = jnp.exp(scores - sums[h])
                gprobs = dot(values, gs[h], NT)
                gscores = (probs * (gprobs - deltas[h]) * scale).astype(BF16)
                gvalue = dot(probs.astype(BF16), gs[h])
                gkey = dot(gscores, qs[h])
                gkeys = gkey if gkeys is None else gkeys + gkey
                gvalues = gvalue if gvalues is None else gvalues + gvalue
                out.append(carry[h] + dot(keys, gscores, TN))
            return tuple(out), gkeys, gvalues

        carry = tuple(jnp.zeros((n, block), F32) for _ in range(heads))
        inner = run // block

        def prev_step(j, carry):
            k, rows = j // inner, pl.ds(pl.multiple_of((j % inner) * block, block), block)
            carry, gkeys, gvalues = step(prev_ref[k, rows, :n], prev_ref[k, rows, n:], carry)
            hold_ref[k, rows, :n] += gkeys
            hold_ref[k, rows, n:] += gvalues
            return carry

        carry = lax.fori_loop(0, place * inner, prev_step, carry)

        def own_step(j, carry):
            rows = pl.ds(pl.multiple_of((j ^ flip) * block, block), block)
            carry, gkeys, gvalues = step(own_ref[rows, :n], own_ref[rows, n:], carry)
            gown_ref[rows, :n] += gkeys
            gown_ref[rows, n:] += gvalues
            return carry

        carry = lax.fori_loop(0, home, own_step, carry)
        limit = diagonal(block, corner, rows_each, length - first)
        rows = pl.ds(pl.multiple_of(i * block, block), block)
        carry, gkeys, gvalues = step(own_ref[rows, :n], own_ref[rows, n:], carry, limit)
        gown_ref[rows, :n] += gkeys
        gown_ref[rows, n:] += gvalues
        gq = jnp.concatenate([carry[h][h * HD : (h + 1) * HD] for h in range(heads)], axis=0).T
        gq_ref[...] = turn(gq, table_ref[...], back=True).astype(BF16)

    @pl.when(i == pl.num_programs(0) - 1)
    def _():
        gprev_ref[...] = hold_ref[...].astype(BF16)


def attend_back(at, q, kv, prev, gatt, res, lse, tables, block, rows_each):
    run, n = q.shape
    heads = n // HD
    before = prev.shape[0]
    shape = jax.ShapeDtypeStruct
    tiles = run * (before * run + run)
    return pl.pallas_call(
        functools.partial(attend_back_kernel, rows_each),
        grid=(run // block,),
        in_specs=[
            pl.BlockSpec(memory_space=pltpu.SMEM),
            rows_of(block, n),
            whole(run, 2 * n),
            whole(before, run, 2 * n),
            rows_of(block, n),
            rows_of(block, n),
            pl.BlockSpec((heads, block), lambda i: (0, i)),
            pl.BlockSpec((3, block, n), lambda i: (0, i, 0)),
        ],
        out_specs=[rows_of(block, n), whole(run, 2 * n), whole(before, run, 2 * n)],
        out_shape=[
            shape((run, n), BF16),
            shape((run, 2 * n), F32),
            shape((before, run, 2 * n), BF16),
        ],
        scratch_shapes=[pltpu.VMEM((before, run, 2 * n), F32)],
        compiler_params=params(),
        cost_estimate=cost(32 * run * (before * run + run) * n),
        name="attend_back",
    )(at, q, kv, prev, gatt, res, lse, tables)


def in_back_kernel(
    gq_ref, gkv_ref, got_ref, gup_ref, w_ref, table_ref, gin_ref, bias_ref, *y_refs
):
    n = gq_ref.shape[1]
    rows = y_refs[0].shape[0]
    half = len(y_refs) // 2
    sums = None
    for part in range(2):
        at = slice(part * half * rows, (part + 1) * half * rows)
        gkv = gkv_ref[at, :]
        for j in range(got_ref.shape[0]):
            gkv = gkv + got_ref[j, at, :].astype(F32)
        gkey = turn(gkv[:, :n], table_ref[:, at], back=True).astype(BF16)
        gin = jnp.concatenate([gq_ref[at, :], gkey, gkv[:, n:].astype(BF16)], axis=1)
        gin_ref[at, :] = gin
        gin = jnp.concatenate([gin, gup_ref[at, :]], axis=1)
        out = dot(gin, w_ref[...], NT).astype(BF16)
        for j in range(half):
            y_refs[part * half + j][...] = out[j * rows : (j + 1) * rows]
        term = jnp.sum(gin.astype(F32), 0, keepdims=True)
        sums = term if sums is None else sums + term
    bias_ref[...] = sums


def in_back(gq, gkv, got, gup, win, tables, rows):
    run, n = gq.shape
    width, wide = win.shape
    shape = jax.ShapeDtypeStruct
    return pl.pallas_call(
        in_back_kernel,
        out_shape=[shape((run, 3 * n), BF16), shape((1, wide), F32)]
        + [shape((rows, width), BF16)] * (run // rows),
        compiler_params=plain(),
        cost_estimate=cost(2 * run * width * wide, 2 * win.size),
        name="in_back",
    )(gq, gkv, got, gup, win, tables)


def weight_grad_kernel(counts, *refs):
    out_ref, hold_ref = refs[-2:]
    first = pl.program_id(0) == 0
    groups = []
    col = at = 0
    for xs, slots, parts in counts:
        groups.append((refs[at : at + xs], refs[at + xs : at + xs + slots * parts], slots, col))
        for j in range(parts):
            col += refs[at + xs + j * slots].shape[1]
        at += xs + slots * parts

    @pl.when(first)
    def _():
        for _, ys, slots, col in groups:
            for j in range(len(ys) // slots):
                for m in range(slots):
                    y_ref = ys[j * slots + m]
                    run, wide = y_ref.shape
                    hold_ref[m * run : (m + 1) * run, col : col + wide] = y_ref[...]
                col += ys[j * slots].shape[1]

    for k, (xs, _, _, col) in enumerate(groups):
        end = groups[k + 1][3] if k + 1 < len(groups) else out_ref.shape[1]
        left = jnp.concatenate([ref[...] for ref in xs], axis=0)
        out_ref[:, col:end] = dot(left, hold_ref[:, col:end], TN).astype(BF16)


def weight_grad(groups, block):
    rows, width = groups[0][0][0].shape
    tokens = rows * len(groups[0][0])
    counts, specs, flat = [], [], []
    for xs, ys in groups:
        counts.append((len(xs), len(ys[0]), len(ys)))
        arrays = [array for part in ys for array in part]
        specs += [pl.BlockSpec((rows, block), lambda i: (0, i)) for _ in xs]
        specs += [whole(*array.shape) for array in arrays]
        flat += [*xs, *arrays]
    wide = sum(part[0].shape[1] for _, ys in groups for part in ys)
    return pl.pallas_call(
        functools.partial(weight_grad_kernel, tuple(counts)),
        grid=(width // block,),
        in_specs=specs,
        out_specs=rows_of(block, wide),
        out_shape=jax.ShapeDtypeStruct((width, wide), BF16),
        scratch_shapes=[pltpu.VMEM((tokens, wide), BF16)],
        compiler_params=params(),
        cost_estimate=cost(2 * tokens * width * wide, 2 * tokens * (width + wide)),
        name="weight_grad",
    )(*flat)


def at_part(index, size):
    return pl.ds(pl.multiple_of(index * size, size), size)


def pack_in_kernel(at_ref, qkv_ref, up_ref, *out_refs):
    count = len(out_refs)
    n, f = qkv_ref.shape[3] // count, up_ref.shape[2] // count
    for k, out_ref in enumerate(out_refs):
        place = (at_ref[0] + k) % count
        for j in range(3):
            out_ref[:, j * n : (j + 1) * n] = qkv_ref[0, j, :, at_part(place, n)]
        out_ref[:, 3 * n :] = up_ref[0, :, at_part(place, f)]


def pack_out_kernel(at_ref, out_w_ref, down_ref, *out_refs):
    count = len(out_refs)
    n, f = out_w_ref.shape[1] // count, down_ref.shape[1] // count
    for k, out_ref in enumerate(out_refs):
        place = (at_ref[0] + k) % count
        out_ref[:, :n] = out_w_ref[0, at_part(place, n), :].astype(F32).T.astype(BF16)
        out_ref[:, n:] = down_ref[0, at_part(place, f), :].astype(F32).T.astype(BF16)


def pack(kernel, at, first, second, layer, shape, count):
    def of_layer(array):
        rest = array.shape[1:]
        return pl.BlockSpec((1, *rest), lambda i: (layer,) + (0,) * len(rest))

    return pl.pallas_call(
        kernel,
        grid=(1,),
        in_specs=[pl.BlockSpec(memory_space=pltpu.SMEM), of_layer(first), of_layer(second)],
        out_specs=[whole(*shape)] * count,
        out_shape=[jax.ShapeDtypeStruct(shape, BF16)] * count,
        compiler_params=params(),
        cost_estimate=COST,
        name="pack",
    )(at, first, second)


def place_kernel(count, at_ref, *refs):
    blocks, out_ref, sems = refs[:count], refs[count], refs[count + 1]
    copies = []
    for k, block_ref in enumerate(blocks):
        rows = pl.ds(pl.multiple_of(at_ref[k], 16), block_ref.shape[0])
        copies.append(pltpu.make_async_copy(block_ref, out_ref.at[rows], sems.at[k]))
    for copy in copies:
        copy.start()
    for copy in copies:
        copy.wait()


def place(rows, blocks):
    count = len(blocks)
    total = sum(block.shape[0] for block in blocks)
    return pl.pallas_call(
        functools.partial(place_kernel, count),
        in_specs=[pl.BlockSpec(memory_space=pltpu.SMEM)]
        + [pl.BlockSpec(memory_space=pltpu.VMEM)] * count,
        out_specs=pl.BlockSpec(memory_space=pl.ANY),
        out_shape=jax.ShapeDtypeStruct((total, blocks[0].shape[1]), BF16),
        scratch_shapes=[pltpu.SemaphoreType.DMA((count,))],
        compiler_params=plain(),
        cost_estimate=COST,
        name="place",
    )(rows, *blocks)


def unpack_qkv_kernel(held, at_ref, *refs):
    blocks, qkv_ref = refs[: -1 - held], refs[-1]
    count = len(blocks)
    n = qkv_ref.shape[3] // count
    for k, block_ref in enumerate(blocks):
        source = (at_ref[0] + count - k) % count
        value = block_ref[...].astype(F32)
        for j in range(3):
            qkv_ref[0, j, :, at_part(source, n)] = value[:, j * n : (j + 1) * n]


def unpack_rest_kernel(held, at_ref, *refs):
    blocks, (out_ref, down_ref, up_ref) = refs[: -3 - held], refs[-3:]
    count = len(blocks)
    n, f = out_ref.shape[1] // count, down_ref.shape[1] // count
    for k, block_ref in enumerate(blocks):
        source = (at_ref[0] + count - k) % count
        value = block_ref[...].astype(F32)
        out_ref[0, at_part(source, n), :] = value[:, :n].T
        down_ref[0, at_part(source, f), :] = value[:, n : n + f].T
        up_ref[0, :, at_part(source, f)] = value[:, n + f :]


def unpack(kernel, at, blocks, layer, shapes, held):
    def of_layer(shape):
        return pl.BlockSpec((1, *shape[1:]), lambda i: (layer,) + (0,) * (len(shape) - 1))

    held = held or []
    first = 1 + len(blocks)
    return pl.pallas_call(
        functools.partial(kernel, len(held)),
        grid=(1,),
        in_specs=[pl.BlockSpec(memory_space=pltpu.SMEM)]
        + [whole(*block.shape) for block in blocks]
        + [pl.BlockSpec(memory_space=pl.ANY) for _ in held],
        out_specs=[of_layer(shape) for shape in shapes],
        out_shape=[jax.ShapeDtypeStruct(shape, F32) for shape in shapes],
        input_output_aliases={first + j: j for j in range(len(held))},
        compiler_params=params(),
        cost_estimate=COST,
        name="unpack",
    )(at, *blocks, *held)


def blocks_in_order(array, outer, inner):
    d = array.shape[-1] // (outer * inner)
    places = [(i * inner + j) * d for j in range(inner) for i in range(outer)]
    return jnp.concatenate([array[..., p : p + d] for p in places], axis=-1)


def first_kernel(S, C, at_ref, x_ref, gain_ref, shift_ref, hidden_ref, *out_refs):
    rows = hidden_ref.shape[0]
    gain, shift = (blocks_in_order(ref[...], S, C) for ref in (gain_ref, shift_ref))
    for b, out_ref in enumerate(out_refs):
        x = x_ref[0, at_part(at_ref[1] ^ b, rows), :].astype(F32)
        x = blocks_in_order(x, S, C)
        if b == 0:
            hidden_ref[...] = x
        out_ref[...] = layer_norm(x, gain, shift).astype(BF16)


def first_norm(at, x, gain, shift, S, C, count):
    rows, width = x.shape[1] // count, x.shape[2]
    shape = jax.ShapeDtypeStruct
    vmem = pl.BlockSpec(memory_space=pltpu.VMEM)
    return pl.pallas_call(
        functools.partial(first_kernel, S, C),
        in_specs=[pl.BlockSpec(memory_space=pltpu.SMEM), vmem, vmem, vmem],
        out_shape=[shape((rows, width), F32)] + [shape((rows, width), BF16)] * count,
        compiler_params=plain(),
        cost_estimate=COST,
        name="first_norm",
    )(at, x, gain[None], shift[None])


def last_kernel(S, C, at_ref, x_ref, grad_ref, *out_refs):
    rows = grad_ref.shape[0]
    for b, out_ref in enumerate(out_refs):
        part = at_ref[1] ^ b
        x = blocks_in_order(x_ref[0, at_part(part, rows), :].astype(F32), S, C)
        at = at_ref[0] * len(out_refs) * rows + part * rows
        at = at + lax.broadcasted_iota(jnp.int32, (rows, 1), 0)
        x = jnp.where(at < at_ref[2], x, 0.0)
        if b == 0:
            grad_ref[...] = x
        out_ref[...] = x.astype(BF16)


def last_grad(at, x, S, C, count):
    rows, width = x.shape[1] // count, x.shape[2]
    shape = jax.ShapeDtypeStruct
    return pl.pallas_call(
        functools.partial(last_kernel, S, C),
        in_specs=[pl.BlockSpec(memory_space=pltpu.SMEM), pl.BlockSpec(memory_space=pltpu.VMEM)],
        out_shape=[shape((rows, width), F32)] + [shape((rows, width), BF16)] * count,
        compiler_params=plain(),
        cost_estimate=COST,
        name="last_grad",
    )(at, x)


def rows_kernel(S, C, at_ref, x_ref, out_ref):
    rows = x_ref.shape[0]
    at = at_ref[0] + lax.broadcasted_iota(jnp.int32, (rows, 1), 0)
    x = jnp.where(at < at_ref[1], x_ref[...].astype(F32), 0.0)
    out_ref[...] = blocks_in_order(x, C, S).astype(BF16)


def rows_out(at, x, S, C):
    return pl.pallas_call(
        functools.partial(rows_kernel, S, C),
        in_specs=[pl.BlockSpec(memory_space=pltpu.SMEM), pl.BlockSpec(memory_space=pltpu.VMEM)],
        out_shape=jax.ShapeDtypeStruct(x.shape, BF16),
        compiler_params=plain(),
        cost_estimate=COST,
        name="rows_out",
    )(at, x)


def norm_kernel(count, S, C, *refs):
    parts = refs[:count]
    hidden_ref, out_ref, down_ref, gain_ref, shift_ref, next_ref, normed_ref = refs[count:]
    hidden = hidden_ref[...] + blocks_in_order(out_ref[...] + down_ref[...], S, C)
    for ref in parts:
        hidden = hidden + ref[...].astype(F32)
    next_ref[...] = hidden
    gain, shift = (blocks_in_order(ref[...], S, C) for ref in (gain_ref, shift_ref))
    normed_ref[...] = layer_norm(hidden, gain, shift).astype(BF16)


def sum_norm(parts, hidden, rows, S, C):
    shape = jax.ShapeDtypeStruct
    return pl.pallas_call(
        functools.partial(norm_kernel, len(parts), S, C),
        out_shape=[shape(hidden.shape, F32), shape(hidden.shape, BF16)],
        compiler_params=plain(),
        cost_estimate=COST,
        name="sum_norm",
    )(*parts, hidden, *[row[None] for row in rows])


def norm_back_kernel(count, S, C, *refs):
    parts = refs[:count]
    hidden_ref, grad_ref, gain_ref, next_ref, low_ref, sums_ref = refs[count:]
    total = parts[0][...].astype(F32)
    for ref in parts[1:]:
        total = total + ref[...].astype(F32)
    hidden = hidden_ref[...]
    centred = hidden - jnp.mean(hidden, -1, keepdims=True)
    factor = lax.rsqrt(jnp.mean(centred * centred, -1, keepdims=True) + 1e-05)
    xhat = centred * factor
    grad = grad_ref[...]
    for j, value in enumerate((total * xhat, total, grad)):
        sums_ref[j : j + 1, :] = blocks_in_order(jnp.sum(value, 0, keepdims=True), C, S)
    inner = total * blocks_in_order(gain_ref[...], S, C)
    first = jnp.mean(inner, -1, keepdims=True)
    second = jnp.mean(inner * xhat, -1, keepdims=True)
    grad = grad + factor * (inner - first - xhat * second)
    next_ref[...] = grad
    low_ref[...] = grad.astype(BF16)


def sum_norm_back(parts, hidden, grad, gain, S, C):
    shape = jax.ShapeDtypeStruct
    return pl.pallas_call(
        functools.partial(norm_back_kernel, len(parts), S, C),
        out_shape=[
            shape(hidden.shape, F32),
            shape(hidden.shape, BF16),
            shape((3, hidden.shape[1]), F32),
        ],
        compiler_params=plain(),
        cost_estimate=COST,
        name="sum_norm_back",
    )(*parts, hidden, grad, gain[None])


class Stages:
    def __init__(self, token):
        self.token = token
        self.active = []
        self.count = 0

    def spawn(self, process):
        self.active.append((process, None))

    def hold(self, *arrays):
        return lax.optimization_barrier((self.token, *arrays))[1:]

    def step(self):
        self.count += 1
        given, moved = [], True
        while moved:
            moved, todo, self.active = False, self.active, []
            for process, value in todo:
                try:
                    out = process.send(value)
                except StopIteration:
                    moved = True
                    continue
                if out is WAIT:
                    self.active.append((process, None))
                else:
                    moved = True
                    given.append((process, out))
        flat, tree = jax.tree.flatten([out for _, out in given])
        flat = lax.optimization_barrier((self.token, *flat))
        self.token = flat[0]
        outs = jax.tree.unflatten(tree, flat[1:])
        self.active += [(process, out) for (process, _), out in zip(given, outs)]

    def run(self):
        while self.active:
            before = [id(process) for process, _ in self.active]
            self.step()
            assert self.count < 500


WAIT = object()


def until(ready):
    while not ready():
        yield WAIT


FAST = [[(1, None), (3, None)], [(2, None)]]
SLOW = [[(1, None)], [(3, None)], [(2, 0)], [(2, 1)]]


class Group:
    def __init__(self):
        self.S = lax.axis_size("slot")
        self.C = lax.axis_size("ctx")
        self.T = lax.axis_size("tp")
        self.s = lax.axis_index("slot")
        self.c = lax.axis_index("ctx")
        self.t = lax.axis_index("tp")
        assert self.S == 4 and self.T == 4
        self.far, self.near = self.T // 2, 1
        self.corner = (self.t % 2) * 2 + self.t // 2
        self.slot_at = self.s.astype(jnp.int32)[None]

    def swap(self, block, bit):
        return lax.ppermute(block, "tp", [(i, i ^ bit) for i in range(self.T)])

    def shift(self, block, k):
        S = self.S
        return lax.ppermute(block, "slot", [(i, (i + k) % S) for i in range(S)])

    def parts_of(self, array, rows):
        return [
            lax.dynamic_slice_in_dim(array, (self.corner ^ b) * rows, rows, 0)
            for b in range(self.T)
        ]

    def in_order(self, parts):
        rows = parts[0].shape[0]
        array = jnp.zeros((self.T * rows, *parts[0].shape[1:]), parts[0].dtype)
        for b, part in enumerate(parts):
            array = lax.dynamic_update_slice_in_dim(array, part, (self.corner ^ b) * rows, 0)
        return array

    def gather(self, block, own_parts, ready, sent=lambda: None):
        blocks = {0: block}
        if own_parts is not None:
            ready(0, own_parts)
        waiting = []
        order = [0, 1, 3, 2]
        for r in range(6):
            for k, parts in waiting:
                ready(k, parts + [self.swap(parts[1], self.near)])
            waiting = []
            if r == 5:
                return
            fresh = {}
            if r == 0:
                fresh[1] = self.shift(block, -1)
            elif r == 1:
                fresh[3] = self.shift(block, 1)
            elif r == 2:
                fresh["down"] = lax.ppermute(blocks[1], "slot", [(1, 0), (2, 1)])
                fresh["up"] = lax.ppermute(blocks[3], "slot", [(1, 2), (2, 3)])
            if r == 3:
                blocks[2] = lax.optimization_barrier(
                    jnp.where(self.s < 2, blocks["down"], blocks["up"])
                )
            if r < 4 and (r > 0 or own_parts is None):
                k = order[r]
                mine = blocks[k]
                parts = [mine, self.swap(mine, self.far), self.swap(mine, self.near)]
                fresh, parts = yield fresh, parts
                waiting = [(k, parts)]
            elif r < 4:
                (fresh,) = yield (fresh,)
            blocks.update(fresh)
            if r == 2:
                sent()

    def scatter(self, make, there, finish):
        order = [2, 1, 3, 0]
        near, far, from_two = {}, {}, {}
        got = []

        def total(k, *more):
            return lax.optimization_barrier(
                sum((a.astype(F32) for a in more), sum(a.astype(F32) for a in far[k])).astype(BF16)
            )

        for r in range(5):
            if r < 4:
                yield from until(lambda: there(order[r]))
            sent = {}
            if r >= 1:
                keep, give = near[order[r - 1]]
                away = (keep[1].astype(F32) + give[1].astype(F32)).astype(BF16)
                sent["far"] = (keep[0], give[0], self.swap(away, self.far))
            if r == 2:
                two = total(2)
                sent["up"] = lax.ppermute(two, "slot", [(0, 1), (1, 2)])
                sent["down"] = lax.ppermute(two, "slot", [(2, 1), (3, 2)])
            if r == 3:
                sent["got"] = self.shift(total(1, from_two["up"]), 1)
            if r == 4:
                sent["got"] = self.shift(total(3, from_two["down"]), -1)
            if r < 4:
                keep0, keep1, give0, give1 = make(order[r])
                sent["near"] = (
                    (keep0, keep1),
                    (self.swap(give0, self.near), self.swap(give1, self.near)),
                )
            sent, got = yield sent, got
            if "near" in sent:
                near[order[r]] = sent["near"]
            if "far" in sent:
                far[order[r - 1]] = sent["far"]
            if "up" in sent:
                from_two = sent
            if "got" in sent:
                got = got + [sent["got"]]
        finish(list(far[0]) + got)

    def ctx_before(self, block):
        C = self.C
        got = [
            lax.ppermute(block, "ctx", [(i, i + j) for i in range(C - j)])[None]
            for j in range(1, C)
        ]
        return got[0] if C == 2 else jnp.concatenate(got)

    def ctx_return(self, blocks):
        C = self.C
        got = [
            lax.ppermute(blocks[j - 1], "ctx", [(i, i - j) for i in range(j, C)])[None]
            for j in range(1, C)
        ]
        return got[0] if C == 2 else jnp.concatenate(got)

    def ctx_others(self, block):
        C = self.C
        return [
            lax.ppermute(block, "ctx", [(i, (i + j) % C) for i in range(C)]) for j in range(1, C)
        ]

    def gather_weights(self, pieces, done, sent, rounds):
        S, C = self.S, self.C
        d, wide = pieces[0].shape
        back = [(pieces[0], 0, 0)]
        blocks, starts = [], []
        rounds = list(rounds)
        while back or rounds:
            shifts = rounds.pop(0) if rounds else []
            parts = []
            for k, part in shifts:
                piece = pieces[k]
                if part is not None:
                    piece = piece[part * d // 2 : (part + 1) * d // 2]
                parts.append((piece, k, 0 if part is None else part * d // 2))
            got = [self.shift(piece, k) for piece, k, _ in parts]
            others = [self.ctx_others(block) for block, _, _ in back]
            got, others, blocks, pieces = yield got, others, blocks, pieces
            blocks = list(blocks)
            for (block, k, row), found in zip(back, others):
                for j, part in enumerate([block] + list(found)):
                    blocks.append(part)
                    starts.append((j, k, row))
            back = [(block, k, row) for block, (_, k, row) in zip(got, parts)]
            if not rounds:
                sent()
        j, k, row = jnp.asarray(starts, jnp.int32).T
        done(place(((self.c - j) % C * S + (self.s - k) % S) * d + row, blocks))

    def gather_weights_later(self, pieces, done, sent, steps):
        S, C = self.S, self.C
        d, wide = pieces[0].shape
        got = []
        for k, piece in ((1, pieces[1]), (3, pieces[3])) + self.halves(pieces[2]):
            got, pieces = yield got + [self.shift(piece, k)], pieces
        sent()
        k, row = jnp.asarray([(0, 0), (1, 0), (3, 0), (2, 0), (2, d // 2)], jnp.int32).T
        flat = place((self.s - k) % S * d + row, [pieces[0], *got])
        array = lax.all_gather(flat, "ctx")
        for _ in range(steps):
            yield ()
        done(array.reshape(C * S * d, wide))

    def halves(self, block):
        half = block.shape[0] // 2
        return ((2, block[:half]), (2, block[half:]))

    def scatter_weights(self, grad, done, steps):
        S, C = self.S, self.C
        wide = grad.shape[1]
        d = grad.shape[0] // (S * C)
        own = lax.psum_scatter(grad.reshape(C, S, d, wide), "ctx")
        for _ in range(steps):
            yield ()
        pieces = [
            lax.dynamic_index_in_dim(own, (self.s + k) % S, 0, keepdims=False) for k in range(S)
        ]
        got = []
        for k, piece in ((1, pieces[1]), (3, pieces[3])) + self.halves(pieces[2]):
            got, pieces = yield got + [self.shift(piece, k)], pieces
        done([pieces[0], got[0], jnp.concatenate(got[2:]), got[1]])

    def scatter_weights_now(self, grad, done, slow=False):
        S, C = self.S, self.C
        wide = grad.shape[1]
        d = grad.shape[0] // (S * C)
        grad = grad.reshape(C, S, d, wide)

        def piece(k, j):
            at = ((self.c + j) % C, (self.s + k) % S, 0, 0)
            return lax.dynamic_slice(grad, at, (1, 1, d, wide)).reshape(d, wide)

        def add(k):
            other = [
                lax.ppermute(piece(k, j), "ctx", [(i, (i + j) % C) for i in range(C)])
                for j in range(1, C)
            ]
            return [piece(k, 0)] + other

        def total(parts):
            value = sum((part.astype(F32) for part in parts[1:]), parts[0].astype(F32))
            return lax.optimization_barrier(value.astype(BF16))

        if slow:
            two, one = yield add(2), add(1)
            low, high = self.halves(total(two))
            low, high, one, three = yield self.shift(low[1], 2), high[1], one, add(3)
            low, high, one, three, own = yield low, self.shift(high, 2), one, three, add(0)
            low, high, one, three, own = yield low, high, self.shift(total(one), 1), three, own
            low, high, one, three, own = yield (
                low, high, one, self.shift(total(three), 3), total(own),
            )
            done([own, one, jnp.concatenate([low, high]), three])
            return
        two, one = yield add(2), add(1)
        two, one, three, own = yield self.shift(total(two), 2), self.shift(total(one), 1), add(3), add(0)
        two, one, three, own = yield two, one, self.shift(total(three), 3), total(own)
        done([own, one, two, three])

    def add_up(self, small, part, finish):
        cut = small.shape[0]
        both = jnp.concatenate([small, part])
        got = [self.shift(both, k) for k in range(1, self.S)]
        got, both = yield got, both
        both = sum(got, both)
        got = self.ctx_others(both)
        got, both = yield got, both
        both = sum(got, both)
        small, part = both[:cut], both[cut:]
        got = [self.swap(small, bit) for bit in range(1, self.T)]
        got, small, part = yield got, small, part
        finish(sum(got, small), part)


def on_device(
    inputs,
    lengths,
    ln_gain,
    ln_shift,
    w_qkv,
    b_qkv,
    w_out,
    b_out,
    w_up,
    b_up,
    w_down,
    b_down,
    cotangent,
):
    grp = Group()
    S, C, T = grp.S, grp.C, grp.T
    _, run, width = inputs.shape
    rows = run // T
    nt, ft = w_qkv.shape[3], w_up.shape[2]
    n, f = nt // S, ft // S
    d = w_up.shape[1]
    block = run // 2
    stages = Stages(lengths)

    here = jnp.concatenate([grp.c[None], grp.corner[None], lengths]).astype(jnp.int32)
    own_at = jnp.concatenate([(grp.c * run + grp.corner * rows)[None], lengths]).astype(jnp.int32)
    local = jnp.arange(run, dtype=jnp.int32)
    positions = grp.c * run + (local // rows ^ grp.corner) * rows + local % rows
    tables = rotary_tables(positions, n // HD)
    box = {}
    kept = [[None] * S for _ in range(LAYERS)]
    normed = [[None] * S for _ in range(LAYERS)]
    grad_branch = [[None] * S for _ in range(LAYERS)]
    middle = [[None] * S for _ in range(LAYERS)]
    gins = [[None] * S for _ in range(LAYERS)]
    bias_sums = [[None] * S for _ in range(LAYERS)]
    small_sums = [None] * LAYERS

    def bias_part(bias, size):
        return lax.dynamic_slice_in_dim(bias, grp.s * size, size, bias.ndim - 1)

    biases = [
        jnp.concatenate([bias_part(b_qkv[layer], n).reshape(-1), bias_part(b_up[layer], f)])[None]
        for layer in range(LAYERS)
    ]
    def after(*keys):
        return until(lambda: all(key in box for key in keys))

    def mark(*key):
        return lambda *value: box.__setitem__(key, value[0] if value else True)

    def lengths_of_all():
        got = yield [grp.shift(lengths, -k) for k in range(1, S)]
        for k, value in enumerate([lengths] + list(got)):
            box["at", k] = jnp.concatenate([value, grp.c[None], grp.corner[None]])

    def in_weights(layer, *keys, later=None):
        yield from after(*keys)
        pieces = pack(
            pack_in_kernel, grp.slot_at, w_qkv, w_up, layer, (d, 3 * n + f), S
        )
        pieces = list(stages.hold(*pieces))
        if later is None:
            yield from grp.gather_weights(
                pieces, mark("win", layer), mark("win sent", layer), FAST if layer == 0 else SLOW
            )
        else:
            yield from grp.gather_weights_later(
                pieces, mark("win", layer), mark("win sent", layer), later
            )

    def out_weights(layer, *keys, later=None):
        yield from after(*keys)
        pieces = pack(pack_out_kernel, grp.slot_at, w_out, w_down, layer, (d, n + f), S)
        pieces = list(stages.hold(*pieces))
        if later is None:
            yield from grp.gather_weights(
                pieces, mark("wout", layer), mark("wout sent", layer), FAST if layer == 0 else SLOW
            )
        else:
            yield from grp.gather_weights_later(
                pieces, mark("wout", layer), mark("wout sent", layer), later
            )

    def forward_slot(layer, k, parts):
        yield from after(("win", layer), ("at", k))
        normed[layer][k] = parts
        q, kv, up, act = in_project(parts, box["win", layer], biases[layer], tables, n)
        prev = grp.ctx_before(kv)
        if k != 2:
            q, kv, up, act = yield q, kv, up, act
        else:
            yield ()
        if k != 2:
            yield ()
        res, att, lse = attend(box["at", k], q, kv, prev, block, rows)
        box["attended", layer, k] = True
        kept[layer][k] = (q, kv, prev, up, act, res, att, lse)

    def make_forward(layer):
        def make(k):
            return out_project(kept[layer][k][6], kept[layer][k][4], box["wout", layer], rows)

        return make

    def there_forward(layer):
        return lambda k: ("attended", layer, k) in box and ("wout", layer) in box

    def backward_slot(layer, k, parts):
        yield from after(("wout", layer), ("attended", layer, k))
        grad_branch[layer][k] = parts
        if all(grad_branch[layer]):
            box["grad gathered", layer] = True
        q, kv, prev, up, _, res, _, lse = kept[layer][k]
        gatt, gup = out_back(parts, box["wout", layer], up, n)
        gq, gkv, gprev = attend_back(
            box["at", k], q, kv, prev, gatt, res, lse, tables, block, rows
        )
        if k == 2:
            got = grp.ctx_return(gprev)
            gq, gkv, gup = yield gq, gkv, gup
        else:
            gq, gkv, gup, gprev = yield gq, gkv, gup, gprev
            gq, gkv, gup, got = yield gq, gkv, gup, grp.ctx_return(gprev)
        middle[layer][k] = (gq, gkv, got, gup)
        box["middle", layer, k] = True

    def make_backward(layer):
        def make(k):
            gq, gkv, got, gup = middle[layer][k]
            gin, bias_sum, *parts = in_back(gq, gkv, got, gup, box["win", layer], tables, rows)
            gins[layer][k] = gin
            bias_sums[layer][k] = bias_sum[0]
            box["gin", layer, k] = True
            return parts

        return make

    def there_backward(layer):
        return lambda k: ("middle", layer, k) in box

    def slot_ready(kind, layer):
        return lambda m, parts: stages.spawn(kind(layer, m, parts))

    def rest_grads(layer, *keys, steps=4):
        yield from after(*keys)
        grad = weight_grad(
            [
                (
                    [part for parts in grad_branch[layer] for part in parts],
                    [[kept[layer][k][6] for k in range(S)], [kept[layer][k][4] for k in range(S)]],
                ),
                (
                    [part for parts in normed[layer] for part in parts],
                    [[middle[layer][k][3] for k in range(S)]],
                ),
            ],
            block,
        )
        yield ()
        if layer == 0:
            yield from grp.scatter_weights_now(grad, mark("grad rest", layer), slow=True)
        else:
            yield from grp.scatter_weights(grad, mark("grad rest", layer), steps)

    def qkv_grads(layer, steps=4):
        yield from after(*[("gin", layer, k) for k in range(S)])
        grad = weight_grad(
            [([part for parts in normed[layer] for part in parts], [gins[layer]])], block
        )
        (grad,) = yield (grad,)
        if layer == 0:
            yield from grp.scatter_weights_now(grad, mark("grad qkv", layer))
        else:
            yield from grp.scatter_weights(grad, mark("grad qkv", layer), steps)

    def first_gather(*keys):
        yield from after(*keys)
        box["hidden", 0], *parts = first_norm(here, inputs, ln_gain[0], ln_shift[0], S, C, T)
        parts = list(stages.hold(*parts))
        yield from grp.gather(
            parts[0], parts, slot_ready(forward_slot, 0), mark("normed sent", 0)
        )

    def next_gather(layer):
        yield from after(("hidden", layer))
        yield from grp.gather(
            box["normed", layer], None, slot_ready(forward_slot, layer), mark("normed sent", layer)
        )

    def forward_sum(layer, *keys):
        yield from after(*keys)

        def finish(parts):
            later = min(layer + 1, LAYERS - 1)
            box["hidden", layer + 1], box["normed", layer + 1] = sum_norm(
                parts,
                box["hidden", layer],
                (b_out[layer], b_down[layer], ln_gain[later], ln_shift[later]),
                S,
                C,
            )

        yield from grp.scatter(make_forward(layer), there_forward(layer), finish)

    def last_gradient(*keys):
        yield from after(*keys)
        box["grad", LAYERS], *parts = last_grad(here, cotangent, S, C, T)
        parts = list(stages.hold(*parts))
        yield from grp.gather(
            parts[0], parts, slot_ready(backward_slot, LAYERS - 1), mark("grad sent", LAYERS)
        )

    def next_gradient(layer):
        yield from after(("grad", layer))
        yield from grp.gather(
            box["grad low", layer],
            None,
            slot_ready(backward_slot, layer - 1),
            mark("grad sent", layer),
        )

    def backward_sum(layer):
        def finish(parts):
            box["grad", layer], box["grad low", layer], small_sums[layer] = sum_norm_back(
                parts, box["hidden", layer], box["grad", layer + 1], ln_gain[layer], S, C
            )

        yield from grp.scatter(make_backward(layer), there_backward(layer), finish)

    def all_sums(*keys):
        yield from after(*keys)
        spread = []
        for layer in range(LAYERS):
            total = sum(bias_sums[layer][1:], bias_sums[layer][0])
            pieces = jnp.zeros((3 * nt + ft,), F32)
            for i in range(3):
                pieces = lax.dynamic_update_slice_in_dim(
                    pieces, total[i * n : (i + 1) * n], i * nt + grp.s * n, 0
                )
            spread.append(
                lax.dynamic_update_slice_in_dim(pieces, total[3 * n :], 3 * nt + grp.s * f, 0)
            )
        yield from grp.add_up(
            jnp.concatenate(small_sums).reshape(-1),
            jnp.concatenate(spread),
            lambda small, part: box.__setitem__("sums", (small, part)),
        )

    def all_rows(key, value, name):
        yield from after(key)
        block = value()
        parts = [block, grp.swap(block, grp.far), grp.swap(block, grp.near)]
        parts = yield parts
        parts = list(parts) + [grp.swap(parts[1], grp.near)]
        starts = (grp.corner ^ jnp.arange(T, dtype=jnp.int32)) * rows
        box[name] = place(starts, parts)[None]

    def final_qkv(layer, *keys):
        yield from after(("grad qkv", layer), *keys)
        box["final qkv", layer] = unpack(
            unpack_qkv_kernel,
            grp.slot_at,
            box["grad qkv", layer],
            layer,
            ((LAYERS, 3, d, nt),),
            box.get(("final qkv", layer + 1)),
        )

    def final_rest(layer, *keys):
        yield from after(("grad rest", layer), *keys)
        box["final rest", layer] = unpack(
            unpack_rest_kernel,
            grp.slot_at,
            box["grad rest", layer],
            layer,
            ((LAYERS, nt, d), (LAYERS, ft, d), (LAYERS, d, ft)),
            box.get(("final rest", layer + 1)),
        )

    last = LAYERS - 1
    stages.spawn(in_weights(0))
    stages.spawn(lengths_of_all())
    stages.spawn(first_gather(("win sent", 0)))
    stages.spawn(forward_sum(0))
    stages.spawn(out_weights(0, ("normed sent", 0)))
    for layer in range(1, LAYERS):
        stages.spawn(in_weights(layer, ("wout", layer - 1)))
        stages.spawn(next_gather(layer))
        if layer < last:
            stages.spawn(forward_sum(layer))
        stages.spawn(out_weights(layer, ("win sent", layer)))
    stages.spawn(last_gradient(("normed sent", last)))
    for layer in reversed(range(LAYERS)):
        stages.spawn(backward_sum(layer))
        if layer > 0:
            stages.spawn(next_gradient(layer))
    stages.spawn(forward_sum(last, ("normed sent", last)))
    for layer in reversed(range(LAYERS)):
        stages.spawn(rest_grads(layer, ("gin", layer, 0 if layer else 1)))
        stages.spawn(qkv_grads(layer))
        stages.spawn(final_qkv(layer, *([] if layer == last else [("final qkv", layer + 1)])))
        stages.spawn(final_rest(layer, *([] if layer == last else [("final rest", layer + 1)])))
    stages.spawn(
        all_rows(
            ("hidden", LAYERS), lambda: rows_out(own_at, box["hidden", LAYERS], S, C), "block out"
        )
    )
    stages.spawn(all_rows(("grad", 0), lambda: rows_out(own_at, box["grad low", 0], S, C), "grad input"))
    stages.spawn(all_sums(("grad", 0)))
    stages.run()

    small, part = box["sums"]
    small = small.reshape(LAYERS, 3, width)
    part = part.reshape(LAYERS, 3 * nt + ft)
    (grad_qkv,) = box["final qkv", 0]
    grad_out, grad_down, grad_up = box["final rest", 0]
    return (
        box["block out"],
        box["grad input"],
        small[:, 0],
        small[:, 1],
        grad_qkv,
        part[:, : 3 * nt].reshape(LAYERS, 3, nt),
        grad_out,
        small[:, 2],
        grad_up,
        part[:, 3 * nt :],
        grad_down,
        small[:, 2],
    )


def solution(mesh):
    return jax.shard_map(
        on_device,
        mesh=mesh,
        in_specs=(
            P("slot", "ctx", None),
            P("slot"),
            P(),
            P(),
            P(None, None, ("slot", "ctx"), "tp"),
            P(None, None, "tp"),
            P(None, "tp", ("slot", "ctx")),
            P(),
            P(None, ("slot", "ctx"), "tp"),
            P(None, "tp"),
            P(None, "tp", ("slot", "ctx")),
            P(),
            P("slot", "ctx", None),
        ),
        out_specs=(
            P("slot", "ctx", None),
            P("slot", "ctx", None),
            P(),
            P(),
            P(None, None, ("slot", "ctx"), "tp"),
            P(None, None, "tp"),
            P(None, "tp", ("slot", "ctx")),
            P(),
            P(None, ("slot", "ctx"), "tp"),
            P(None, "tp"),
            P(None, "tp", ("slot", "ctx")),
            P(),
        ),
        check_vma=False,
    )
```

```python
import functools
import math

import jax
import jax.numpy as jnp
from jax import lax
from jax.experimental import pallas as pl
from jax.experimental.pallas import tpu as pltpu
from jax.sharding import PartitionSpec as P

HD = 64
ROT = 32
LAYERS = 2

masked = -1e30
F32 = jnp.float32
BF16 = jnp.bfloat16
NT = (((1,), (1,)), ((), ()))
TN = (((0,), (0,)), ((), ()))
VMEM_LIMIT = 20 * 1024 * 1024


def dot(a, b, dims=None):
    if dims is None:
        return jnp.dot(a, b, preferred_element_type=F32)
    return lax.dot_general(a, b, dims, preferred_element_type=F32)


def gelu_tanh(value):
    inner = 0.7978845608028654 * (value + 0.044715 * value * value * value)
    return 0.5 * value * (1.0 + jnp.tanh(inner))


def gelu_slope(value):
    square = value * value
    inner = 0.7978845608028654 * (value + 0.044715 * value * square)
    bend = jnp.tanh(inner)
    slope = 0.7978845608028654 * (1.0 + 3.0 * 0.044715 * square)
    return 0.5 * (1.0 + bend) + 0.5 * value * (1.0 - bend * bend) * slope


def layer_norm(hidden, gain, shift):
    centre = jnp.mean(hidden, -1, keepdims=True)
    centred = hidden - centre
    variance = jnp.mean(centred * centred, -1, keepdims=True)
    return centred * lax.rsqrt(variance + 1e-05) * gain + shift


def rotary_tables(positions, heads):
    half_rot = ROT // 2
    freqs = jnp.exp(jnp.arange(half_rot, dtype=F32) * (-2.0 * math.log(10000.0) / ROT))
    angles = positions.astype(F32)[:, None] * freqs[None, :]
    cosine, sine = jnp.cos(angles), jnp.sin(angles)
    rows = positions.shape[0]
    rest = jnp.zeros((rows, HD - ROT), F32)
    none = jnp.zeros_like(sine)
    same = jnp.concatenate([cosine, cosine, rest + 1.0], axis=1)
    ahead = jnp.concatenate([-sine, none, rest], axis=1)
    behind = jnp.concatenate([none, sine, rest], axis=1)
    return jnp.stack([jnp.tile(part, (1, heads)) for part in (same, ahead, behind)])


def turn(value, tables, back=False):
    width = value.shape[1]
    half_rot = ROT // 2
    moved = (
        pltpu.roll(value, width - half_rot, 1) * tables[1] + pltpu.roll(value, half_rot, 1) * tables[2]
    )
    stay = value * tables[0]
    return stay - moved if back else stay + moved


def in_kernel(count, *refs):
    xs = refs[:count]
    w_ref, bias_ref, table_ref, q_ref, kv_ref, up_ref, act_ref = refs[count:]
    n = q_ref.shape[1]
    rows = xs[0].shape[0]
    half = count // 2
    for part in range(2):
        at = slice(part * half * rows, (part + 1) * half * rows)
        x = jnp.concatenate([ref[...] for ref in xs[part * half : (part + 1) * half]], axis=0)
        out = dot(x, w_ref[...]) + bias_ref[...]
        tables = table_ref[:, at]
        q_ref[at, :] = turn(out[:, :n], tables).astype(BF16)
        kv_ref[at, :n] = turn(out[:, n : 2 * n], tables).astype(BF16)
        kv_ref[at, n:] = out[:, 2 * n : 3 * n].astype(BF16)
        up = out[:, 3 * n :]
        up_ref[at, :] = up
        act_ref[at, :] = gelu_tanh(up).astype(BF16)


def rows_of(block, width):
    return pl.BlockSpec((block, width), lambda i: (i, 0))


def whole(*shape):
    return pl.BlockSpec(shape, lambda i: (0,) * len(shape))


def params():
    return pltpu.CompilerParams(
        dimension_semantics=("arbitrary",), vmem_limit_bytes=VMEM_LIMIT
    )


def plain():
    return pltpu.CompilerParams(vmem_limit_bytes=VMEM_LIMIT)


def cost(flops, moved=0):
    return pl.CostEstimate(
        flops=int(COST_SCALE * flops), bytes_accessed=int(moved), transcendentals=0
    )


COST_SCALE = 1.5
COST = cost(1000)


def in_project(xs, win, bias, tables, n):
    rows, width = xs[0].shape
    run = rows * len(xs)
    f = win.shape[1] - 3 * n
    shape = jax.ShapeDtypeStruct
    return pl.pallas_call(
        functools.partial(in_kernel, len(xs)),
        out_shape=[
            shape((run, n), BF16),
            shape((run, 2 * n), BF16),
            shape((run, f), F32),
            shape((run, f), BF16),
        ],
        compiler_params=plain(),
        cost_estimate=cost(2 * run * width * win.shape[1], 2 * win.size),
        name="in_project",
    )(*xs, win, bias, tables)


def diagonal(block, corner, rows_each, room):
    key = lax.broadcasted_iota(jnp.int32, (block, block), 0)
    query = lax.broadcasted_iota(jnp.int32, (1, block), 1)
    inside = corner % (block // rows_each)

    def at(row):
        return (row // rows_each ^ inside) * rows_each + row % rows_each

    return at(key) < jnp.minimum(at(query) + 1, room)


def attend_kernel(rows_each, at_ref, q_ref, own_ref, prev_ref, res_ref, att_ref, lse_ref):
    length, place, corner = at_ref[0], at_ref[1], at_ref[2]
    block, n = q_ref.shape
    heads = n // HD
    run = own_ref.shape[0]
    i = pl.program_id(0)
    flip = corner * rows_each // block
    home = i ^ flip
    first = place * run + home * block

    @pl.when(first >= length)
    def _():
        res_ref[...] = jnp.zeros_like(res_ref)
        att_ref[...] = jnp.zeros_like(att_ref)
        lse_ref[...] = jnp.zeros_like(lse_ref)

    @pl.when(first < length)
    def _():
        lane = lax.broadcasted_iota(jnp.int32, (1, n), 1)
        q = q_ref[...].astype(F32) * HD ** (-0.5)
        qs = [jnp.where(lane // HD == h, q, 0.0).astype(BF16) for h in range(heads)]

        def step(keys, values, carry, limit=None):
            out = []
            for h in range(heads):
                top, total, accum = carry[h]
                scores = dot(keys, qs[h], NT)
                if limit is not None:
                    scores = jnp.where(limit, scores, masked)
                new_top = jnp.maximum(top, jnp.max(scores, 0, keepdims=True))
                probs = jnp.exp(scores - new_top)
                shrink = jnp.exp(top - new_top)
                total = total * shrink + jnp.sum(probs, 0, keepdims=True)
                accum = accum * shrink + dot(values, probs.astype(BF16), TN)
                out.append((new_top, total, accum))
            return tuple(out)

        carry = tuple(
            (
                jnp.full((1, block), masked, F32),
                jnp.zeros((1, block), F32),
                jnp.zeros((n, block), F32),
            )
            for _ in range(heads)
        )
        inner = run // block

        def prev_step(j, carry):
            rows = pl.ds(pl.multiple_of((j % inner) * block, block), block)
            return step(prev_ref[j // inner, rows, :n], prev_ref[j // inner, rows, n:], carry)

        carry = lax.fori_loop(0, place * inner, prev_step, carry)

        def own_step(j, carry):
            rows = pl.ds(pl.multiple_of((j ^ flip) * block, block), block)
            return step(own_ref[rows, :n], own_ref[rows, n:], carry)

        carry = lax.fori_loop(0, home, own_step, carry)
        limit = diagonal(block, corner, rows_each, length - first)
        rows = pl.ds(pl.multiple_of(i * block, block), block)
        carry = step(own_ref[rows, :n], own_ref[rows, n:], carry, limit)
        parts = []
        for h in range(heads):
            top, total, accum = carry[h]
            lse_ref[h : h + 1, :] = top + jnp.log(total)
            parts.append(accum[h * HD : (h + 1) * HD] / total)
        result = jnp.concatenate(parts, axis=0).T
        res_ref[...] = result
        att_ref[...] = result.astype(BF16)


def attend(at, q, kv, prev, block, rows_each):
    run, n = q.shape
    heads = n // HD
    before = prev.shape[0]
    shape = jax.ShapeDtypeStruct
    tiles = run * (before * run + run)
    return pl.pallas_call(
        functools.partial(attend_kernel, rows_each),
        grid=(run // block,),
        in_specs=[
            pl.BlockSpec(memory_space=pltpu.SMEM),
            rows_of(block, n),
            whole(run, 2 * n),
            whole(before, run, 2 * n),
        ],
        out_specs=[
            rows_of(block, n),
            rows_of(block, n),
            pl.BlockSpec((heads, block), lambda i: (0, i)),
        ],
        out_shape=[shape((run, n), F32), shape((run, n), BF16), shape((heads, run), F32)],
        compiler_params=params(),
        cost_estimate=cost(32 * run * (before * run + run) * n),
        name="attend",
    )(at, q, kv, prev)


def out_kernel(att_ref, act_ref, w_ref, *y_refs):
    rows = y_refs[0].shape[0]
    half = len(y_refs) // 2
    for part in range(2):
        at = slice(part * half * rows, (part + 1) * half * rows)
        both = jnp.concatenate([att_ref[at, :], act_ref[at, :]], axis=1)
        out = dot(both, w_ref[...], NT).astype(BF16)
        for j in range(half):
            y_refs[part * half + j][...] = out[j * rows : (j + 1) * rows]


def out_project(att, act, wout, rows):
    count = att.shape[0] // rows
    return pl.pallas_call(
        out_kernel,
        out_shape=[jax.ShapeDtypeStruct((rows, wout.shape[0]), BF16)] * count,
        compiler_params=plain(),
        cost_estimate=cost(2 * att.shape[0] * wout.size, 2 * wout.size),
        name="out_project",
    )(att, act, wout)


def out_back_kernel(count, *refs):
    xs = refs[:count]
    w_ref, up_ref, gatt_ref, gup_ref = refs[count:]
    n = gatt_ref.shape[1]
    rows = xs[0].shape[0]
    half = count // 2
    for part in range(2):
        at = slice(part * half * rows, (part + 1) * half * rows)
        x = jnp.concatenate([ref[...] for ref in xs[part * half : (part + 1) * half]], axis=0)
        out = dot(x, w_ref[...])
        gatt_ref[at, :] = out[:, :n].astype(BF16)
        gup_ref[at, :] = (out[:, n:] * gelu_slope(up_ref[at, :])).astype(BF16)


def out_back(xs, wout, up, n):
    run, f = up.shape
    shape = jax.ShapeDtypeStruct
    return pl.pallas_call(
        functools.partial(out_back_kernel, len(xs)),
        out_shape=[shape((run, n), BF16), shape((run, f), BF16)],
        compiler_params=plain(),
        cost_estimate=cost(2 * run * wout.size, 2 * wout.size),
        name="out_back",
    )(*xs, wout, up)


def attend_back_kernel(
    rows_each, at_ref, q_ref, own_ref, prev_ref, gatt_ref, res_ref, lse_ref, table_ref,
    gq_ref, gown_ref, gprev_ref, hold_ref,
):
    length, place, corner = at_ref[0], at_ref[1], at_ref[2]
    block, n = q_ref.shape
    heads = n // HD
    run = own_ref.shape[0]
    before = prev_ref.shape[0]
    i = pl.program_id(0)
    flip = corner * rows_each // block
    home = i ^ flip
    first = place * run + home * block

    @pl.when(i == 0)
    def _():
        gown_ref[...] = jnp.zeros_like(gown_ref)
        hold_ref[...] = jnp.zeros_like(hold_ref)

    @pl.when(first >= length)
    def _():
        gq_ref[...] = jnp.zeros_like(gq_ref)

    @pl.when(first < length)
    def _():
        lane = lax.broadcasted_iota(jnp.int32, (1, n), 1)
        q, gatt = q_ref[...], gatt_ref[...]
        pick = [lane // HD == h for h in range(heads)]
        zero = jnp.zeros((), BF16)
        qs = [jnp.where(p, q, zero) for p in pick]
        gs = [jnp.where(p, gatt, zero) for p in pick]
        shared = (gatt.astype(F32) * res_ref[...]).T
        deltas = [jnp.sum(shared[h * HD : (h + 1) * HD], 0, keepdims=True) for h in range(heads)]
        sums = [lse_ref[h : h + 1, :] for h in range(heads)]
        scale = HD ** (-0.5)

        def step(keys, values, carry, limit=None):
            gkeys = gvalues = None
            out = []
            for h in range(heads):
                scores = dot(keys, qs[h], NT) * scale
                if limit is not None:
                    scores = jnp.where(limit, scores, masked)
                probs = jnp.exp(scores - sums[h])
                gprobs = dot(values, gs[h], NT)
                gscores = (probs * (gprobs - deltas[h]) * scale).astype(BF16)
                gvalue = dot(probs.astype(BF16), gs[h])
                gkey = dot(gscores, qs[h])
                gkeys = gkey if gkeys is None else gkeys + gkey
                gvalues = gvalue if gvalues is None else gvalues + gvalue
                out.append(carry[h] + dot(keys, gscores, TN))
            return tuple(out), gkeys, gvalues

        carry = tuple(jnp.zeros((n, block), F32) for _ in range(heads))
        inner = run // block

        def prev_step(j, carry):
            k, rows = j // inner, pl.ds(pl.multiple_of((j % inner) * block, block), block)
            carry, gkeys, gvalues = step(prev_ref[k, rows, :n], prev_ref[k, rows, n:], carry)
            hold_ref[k, rows, :n] += gkeys
            hold_ref[k, rows, n:] += gvalues
            return carry

        carry = lax.fori_loop(0, place * inner, prev_step, carry)

        def own_step(j, carry):
            rows = pl.ds(pl.multiple_of((j ^ flip) * block, block), block)
            carry, gkeys, gvalues = step(own_ref[rows, :n], own_ref[rows, n:], carry)
            gown_ref[rows, :n] += gkeys
            gown_ref[rows, n:] += gvalues
            return carry

        carry = lax.fori_loop(0, home, own_step, carry)
        limit = diagonal(block, corner, rows_each, length - first)
        rows = pl.ds(pl.multiple_of(i * block, block), block)
        carry, gkeys, gvalues = step(own_ref[rows, :n], own_ref[rows, n:], carry, limit)
        gown_ref[rows, :n] += gkeys
        gown_ref[rows, n:] += gvalues
        gq = jnp.concatenate([carry[h][h * HD : (h + 1) * HD] for h in range(heads)], axis=0).T
        gq_ref[...] = turn(gq, table_ref[...], back=True).astype(BF16)

    @pl.when(i == pl.num_programs(0) - 1)
    def _():
        gprev_ref[...] = hold_ref[...].astype(BF16)


def attend_back(at, q, kv, prev, gatt, res, lse, tables, block, rows_each):
    run, n = q.shape
    heads = n // HD
    before = prev.shape[0]
    shape = jax.ShapeDtypeStruct
    tiles = run * (before * run + run)
    return pl.pallas_call(
        functools.partial(attend_back_kernel, rows_each),
        grid=(run // block,),
        in_specs=[
            pl.BlockSpec(memory_space=pltpu.SMEM),
            rows_of(block, n),
            whole(run, 2 * n),
            whole(before, run, 2 * n),
            rows_of(block, n),
            rows_of(block, n),
            pl.BlockSpec((heads, block), lambda i: (0, i)),
            pl.BlockSpec((3, block, n), lambda i: (0, i, 0)),
        ],
        out_specs=[rows_of(block, n), whole(run, 2 * n), whole(before, run, 2 * n)],
        out_shape=[
            shape((run, n), BF16),
            shape((run, 2 * n), F32),
            shape((before, run, 2 * n), BF16),
        ],
        scratch_shapes=[pltpu.VMEM((before, run, 2 * n), F32)],
        compiler_params=params(),
        cost_estimate=cost(32 * run * (before * run + run) * n),
        name="attend_back",
    )(at, q, kv, prev, gatt, res, lse, tables)


def in_back_kernel(
    gq_ref, gkv_ref, got_ref, gup_ref, w_ref, table_ref, gin_ref, bias_ref, *y_refs
):
    n = gq_ref.shape[1]
    rows = y_refs[0].shape[0]
    half = len(y_refs) // 2
    sums = None
    for part in range(2):
        at = slice(part * half * rows, (part + 1) * half * rows)
        gkv = gkv_ref[at, :]
        for j in range(got_ref.shape[0]):
            gkv = gkv + got_ref[j, at, :].astype(F32)
        gkey = turn(gkv[:, :n], table_ref[:, at], back=True).astype(BF16)
        gin = jnp.concatenate([gq_ref[at, :], gkey, gkv[:, n:].astype(BF16)], axis=1)
        gin_ref[at, :] = gin
        gin = jnp.concatenate([gin, gup_ref[at, :]], axis=1)
        out = dot(gin, w_ref[...], NT).astype(BF16)
        for j in range(half):
            y_refs[part * half + j][...] = out[j * rows : (j + 1) * rows]
        term = jnp.sum(gin.astype(F32), 0, keepdims=True)
        sums = term if sums is None else sums + term
    bias_ref[...] = sums


def in_back(gq, gkv, got, gup, win, tables, rows):
    run, n = gq.shape
    width, wide = win.shape
    shape = jax.ShapeDtypeStruct
    return pl.pallas_call(
        in_back_kernel,
        out_shape=[shape((run, 3 * n), BF16), shape((1, wide), F32)]
        + [shape((rows, width), BF16)] * (run // rows),
        compiler_params=plain(),
        cost_estimate=cost(2 * run * width * wide, 2 * win.size),
        name="in_back",
    )(gq, gkv, got, gup, win, tables)


def weight_grad_kernel(counts, *refs):
    out_ref, hold_ref = refs[-2:]
    first = pl.program_id(0) == 0
    groups = []
    col = at = 0
    for xs, slots, parts in counts:
        groups.append((refs[at : at + xs], refs[at + xs : at + xs + slots * parts], slots, col))
        for j in range(parts):
            col += refs[at + xs + j * slots].shape[1]
        at += xs + slots * parts

    @pl.when(first)
    def _():
        for _, ys, slots, col in groups:
            for j in range(len(ys) // slots):
                for m in range(slots):
                    y_ref = ys[j * slots + m]
                    run, wide = y_ref.shape
                    hold_ref[m * run : (m + 1) * run, col : col + wide] = y_ref[...]
                col += ys[j * slots].shape[1]

    for k, (xs, _, _, col) in enumerate(groups):
        end = groups[k + 1][3] if k + 1 < len(groups) else out_ref.shape[1]
        left = jnp.concatenate([ref[...] for ref in xs], axis=0)
        out_ref[:, col:end] = dot(left, hold_ref[:, col:end], TN).astype(BF16)


def weight_grad(groups, block):
    rows, width = groups[0][0][0].shape
    tokens = rows * len(groups[0][0])
    counts, specs, flat = [], [], []
    for xs, ys in groups:
        counts.append((len(xs), len(ys[0]), len(ys)))
        arrays = [array for part in ys for array in part]
        specs += [pl.BlockSpec((rows, block), lambda i: (0, i)) for _ in xs]
        specs += [whole(*array.shape) for array in arrays]
        flat += [*xs, *arrays]
    wide = sum(part[0].shape[1] for _, ys in groups for part in ys)
    return pl.pallas_call(
        functools.partial(weight_grad_kernel, tuple(counts)),
        grid=(width // block,),
        in_specs=specs,
        out_specs=rows_of(block, wide),
        out_shape=jax.ShapeDtypeStruct((width, wide), BF16),
        scratch_shapes=[pltpu.VMEM((tokens, wide), BF16)],
        compiler_params=params(),
        cost_estimate=cost(2 * tokens * width * wide, 2 * tokens * (width + wide)),
        name="weight_grad",
    )(*flat)


def at_part(index, size):
    return pl.ds(pl.multiple_of(index * size, size), size)


def pack_in_kernel(at_ref, qkv_ref, up_ref, *out_refs):
    count = len(out_refs)
    n, f = qkv_ref.shape[3] // count, up_ref.shape[2] // count
    for k, out_ref in enumerate(out_refs):
        place = (at_ref[0] + k) % count
        for j in range(3):
            out_ref[:, j * n : (j + 1) * n] = qkv_ref[0, j, :, at_part(place, n)]
        out_ref[:, 3 * n :] = up_ref[0, :, at_part(place, f)]


def pack_out_kernel(at_ref, out_w_ref, down_ref, *out_refs):
    count = len(out_refs)
    n, f = out_w_ref.shape[1] // count, down_ref.shape[1] // count
    for k, out_ref in enumerate(out_refs):
        place = (at_ref[0] + k) % count
        out_ref[:, :n] = out_w_ref[0, at_part(place, n), :].astype(F32).T.astype(BF16)
        out_ref[:, n:] = down_ref[0, at_part(place, f), :].astype(F32).T.astype(BF16)


def pack(kernel, at, first, second, layer, shape, count):
    def of_layer(array):
        rest = array.shape[1:]
        return pl.BlockSpec((1, *rest), lambda i: (layer,) + (0,) * len(rest))

    return pl.pallas_call(
        kernel,
        grid=(1,),
        in_specs=[pl.BlockSpec(memory_space=pltpu.SMEM), of_layer(first), of_layer(second)],
        out_specs=[whole(*shape)] * count,
        out_shape=[jax.ShapeDtypeStruct(shape, BF16)] * count,
        compiler_params=params(),
        cost_estimate=COST,
        name="pack",
    )(at, first, second)


def place_kernel(count, at_ref, *refs):
    blocks, out_ref, sems = refs[:count], refs[count], refs[count + 1]
    copies = []
    for k, block_ref in enumerate(blocks):
        rows = pl.ds(pl.multiple_of(at_ref[k], 16), block_ref.shape[0])
        copies.append(pltpu.make_async_copy(block_ref, out_ref.at[rows], sems.at[k]))
    for copy in copies:
        copy.start()
    for copy in copies:
        copy.wait()


def place(rows, blocks):
    count = len(blocks)
    total = sum(block.shape[0] for block in blocks)
    return pl.pallas_call(
        functools.partial(place_kernel, count),
        in_specs=[pl.BlockSpec(memory_space=pltpu.SMEM)]
        + [pl.BlockSpec(memory_space=pltpu.VMEM)] * count,
        out_specs=pl.BlockSpec(memory_space=pl.ANY),
        out_shape=jax.ShapeDtypeStruct((total, blocks[0].shape[1]), BF16),
        scratch_shapes=[pltpu.SemaphoreType.DMA((count,))],
        compiler_params=plain(),
        cost_estimate=COST,
        name="place",
    )(rows, *blocks)


def unpack_qkv_kernel(held, at_ref, *refs):
    blocks, qkv_ref = refs[: -1 - held], refs[-1]
    count = len(blocks)
    n = qkv_ref.shape[3] // count
    for k, block_ref in enumerate(blocks):
        source = (at_ref[0] + count - k) % count
        value = block_ref[...].astype(F32)
        for j in range(3):
            qkv_ref[0, j, :, at_part(source, n)] = value[:, j * n : (j + 1) * n]


def unpack_rest_kernel(held, at_ref, *refs):
    blocks, (out_ref, down_ref, up_ref) = refs[: -3 - held], refs[-3:]
    count = len(blocks)
    n, f = out_ref.shape[1] // count, down_ref.shape[1] // count
    for k, block_ref in enumerate(blocks):
        source = (at_ref[0] + count - k) % count
        value = block_ref[...].astype(F32)
        out_ref[0, at_part(source, n), :] = value[:, :n].T
        down_ref[0, at_part(source, f), :] = value[:, n : n + f].T
        up_ref[0, :, at_part(source, f)] = value[:, n + f :]


def unpack(kernel, at, blocks, layer, shapes, held):
    def of_layer(shape):
        return pl.BlockSpec((1, *shape[1:]), lambda i: (layer,) + (0,) * (len(shape) - 1))

    held = held or []
    first = 1 + len(blocks)
    return pl.pallas_call(
        functools.partial(kernel, len(held)),
        grid=(1,),
        in_specs=[pl.BlockSpec(memory_space=pltpu.SMEM)]
        + [whole(*block.shape) for block in blocks]
        + [pl.BlockSpec(memory_space=pl.ANY) for _ in held],
        out_specs=[of_layer(shape) for shape in shapes],
        out_shape=[jax.ShapeDtypeStruct(shape, F32) for shape in shapes],
        input_output_aliases={first + j: j for j in range(len(held))},
        compiler_params=params(),
        cost_estimate=COST,
        name="unpack",
    )(at, *blocks, *held)


def blocks_in_order(array, outer, inner):
    d = array.shape[-1] // (outer * inner)
    places = [(i * inner + j) * d for j in range(inner) for i in range(outer)]
    return jnp.concatenate([array[..., p : p + d] for p in places], axis=-1)


def first_kernel(S, C, at_ref, x_ref, gain_ref, shift_ref, hidden_ref, *out_refs):
    rows = hidden_ref.shape[0]
    gain, shift = (blocks_in_order(ref[...], S, C) for ref in (gain_ref, shift_ref))
    for b, out_ref in enumerate(out_refs):
        x = x_ref[0, at_part(at_ref[1] ^ b, rows), :].astype(F32)
        x = blocks_in_order(x, S, C)
        if b == 0:
            hidden_ref[...] = x
        out_ref[...] = layer_norm(x, gain, shift).astype(BF16)


def first_norm(at, x, gain, shift, S, C, count):
    rows, width = x.shape[1] // count, x.shape[2]
    shape = jax.ShapeDtypeStruct
    vmem = pl.BlockSpec(memory_space=pltpu.VMEM)
    return pl.pallas_call(
        functools.partial(first_kernel, S, C),
        in_specs=[pl.BlockSpec(memory_space=pltpu.SMEM), vmem, vmem, vmem],
        out_shape=[shape((rows, width), F32)] + [shape((rows, width), BF16)] * count,
        compiler_params=plain(),
        cost_estimate=COST,
        name="first_norm",
    )(at, x, gain[None], shift[None])


def last_kernel(S, C, at_ref, x_ref, grad_ref, *out_refs):
    rows = grad_ref.shape[0]
    for b, out_ref in enumerate(out_refs):
        part = at_ref[1] ^ b
        x = blocks_in_order(x_ref[0, at_part(part, rows), :].astype(F32), S, C)
        at = at_ref[0] * len(out_refs) * rows + part * rows
        at = at + lax.broadcasted_iota(jnp.int32, (rows, 1), 0)
        x = jnp.where(at < at_ref[2], x, 0.0)
        if b == 0:
            grad_ref[...] = x
        out_ref[...] = x.astype(BF16)


def last_grad(at, x, S, C, count):
    rows, width = x.shape[1] // count, x.shape[2]
    shape = jax.ShapeDtypeStruct
    return pl.pallas_call(
        functools.partial(last_kernel, S, C),
        in_specs=[pl.BlockSpec(memory_space=pltpu.SMEM), pl.BlockSpec(memory_space=pltpu.VMEM)],
        out_shape=[shape((rows, width), F32)] + [shape((rows, width), BF16)] * count,
        compiler_params=plain(),
        cost_estimate=COST,
        name="last_grad",
    )(at, x)


def rows_kernel(S, C, at_ref, x_ref, out_ref):
    rows = x_ref.shape[0]
    at = at_ref[0] + lax.broadcasted_iota(jnp.int32, (rows, 1), 0)
    x = jnp.where(at < at_ref[1], x_ref[...].astype(F32), 0.0)
    out_ref[...] = blocks_in_order(x, C, S).astype(BF16)


def rows_out(at, x, S, C):
    return pl.pallas_call(
        functools.partial(rows_kernel, S, C),
        in_specs=[pl.BlockSpec(memory_space=pltpu.SMEM), pl.BlockSpec(memory_space=pltpu.VMEM)],
        out_shape=jax.ShapeDtypeStruct(x.shape, BF16),
        compiler_params=plain(),
        cost_estimate=COST,
        name="rows_out",
    )(at, x)


def norm_kernel(count, S, C, *refs):
    parts = refs[:count]
    hidden_ref, out_ref, down_ref, gain_ref, shift_ref, next_ref, normed_ref = refs[count:]
    hidden = hidden_ref[...] + blocks_in_order(out_ref[...] + down_ref[...], S, C)
    for ref in parts:
        hidden = hidden + ref[...].astype(F32)
    next_ref[...] = hidden
    gain, shift = (blocks_in_order(ref[...], S, C) for ref in (gain_ref, shift_ref))
    normed_ref[...] = layer_norm(hidden, gain, shift).astype(BF16)


def sum_norm(parts, hidden, rows, S, C):
    shape = jax.ShapeDtypeStruct
    return pl.pallas_call(
        functools.partial(norm_kernel, len(parts), S, C),
        out_shape=[shape(hidden.shape, F32), shape(hidden.shape, BF16)],
        compiler_params=plain(),
        cost_estimate=COST,
        name="sum_norm",
    )(*parts, hidden, *[row[None] for row in rows])


def norm_back_kernel(count, S, C, *refs):
    parts = refs[:count]
    hidden_ref, grad_ref, gain_ref, next_ref, low_ref, sums_ref = refs[count:]
    total = parts[0][...].astype(F32)
    for ref in parts[1:]:
        total = total + ref[...].astype(F32)
    hidden = hidden_ref[...]
    centred = hidden - jnp.mean(hidden, -1, keepdims=True)
    factor = lax.rsqrt(jnp.mean(centred * centred, -1, keepdims=True) + 1e-05)
    xhat = centred * factor
    grad = grad_ref[...]
    for j, value in enumerate((total * xhat, total, grad)):
        sums_ref[j : j + 1, :] = blocks_in_order(jnp.sum(value, 0, keepdims=True), C, S)
    inner = total * blocks_in_order(gain_ref[...], S, C)
    first = jnp.mean(inner, -1, keepdims=True)
    second = jnp.mean(inner * xhat, -1, keepdims=True)
    grad = grad + factor * (inner - first - xhat * second)
    next_ref[...] = grad
    low_ref[...] = grad.astype(BF16)


def sum_norm_back(parts, hidden, grad, gain, S, C):
    shape = jax.ShapeDtypeStruct
    return pl.pallas_call(
        functools.partial(norm_back_kernel, len(parts), S, C),
        out_shape=[
            shape(hidden.shape, F32),
            shape(hidden.shape, BF16),
            shape((3, hidden.shape[1]), F32),
        ],
        compiler_params=plain(),
        cost_estimate=COST,
        name="sum_norm_back",
    )(*parts, hidden, grad, gain[None])


class Stages:
    def __init__(self, token):
        self.token = token
        self.active = []
        self.count = 0

    def spawn(self, process):
        self.active.append((process, None))

    def hold(self, *arrays):
        return lax.optimization_barrier((self.token, *arrays))[1:]

    def step(self):
        self.count += 1
        given, moved = [], True
        while moved:
            moved, todo, self.active = False, self.active, []
            for process, value in todo:
                try:
                    out = process.send(value)
                except StopIteration:
                    moved = True
                    continue
                if out is WAIT:
                    self.active.append((process, None))
                else:
                    moved = True
                    given.append((process, out))
        flat, tree = jax.tree.flatten([out for _, out in given])
        flat = lax.optimization_barrier((self.token, *flat))
        self.token = flat[0]
        outs = jax.tree.unflatten(tree, flat[1:])
        self.active += [(process, out) for (process, _), out in zip(given, outs)]

    def run(self):
        while self.active:
            before = [id(process) for process, _ in self.active]
            self.step()
            assert self.count < 500


WAIT = object()


def until(ready):
    while not ready():
        yield WAIT


FAST = [[(1, None), (3, None)], [(2, None)]]
SLOW = [[(1, None)], [(3, None)], [(2, 0)], [(2, 1)]]


class Group:
    def __init__(self):
        self.S = lax.axis_size("slot")
        self.C = lax.axis_size("ctx")
        self.T = lax.axis_size("tp")
        self.s = lax.axis_index("slot")
        self.c = lax.axis_index("ctx")
        self.t = lax.axis_index("tp")
        assert self.S == 4 and self.T == 4
        self.far, self.near = self.T // 2, 1
        self.corner = (self.t % 2) * 2 + self.t // 2
        self.slot_at = self.s.astype(jnp.int32)[None]

    def swap(self, block, bit):
        return lax.ppermute(block, "tp", [(i, i ^ bit) for i in range(self.T)])

    def shift(self, block, k):
        S = self.S
        return lax.ppermute(block, "slot", [(i, (i + k) % S) for i in range(S)])

    def parts_of(self, array, rows):
        return [
            lax.dynamic_slice_in_dim(array, (self.corner ^ b) * rows, rows, 0)
            for b in range(self.T)
        ]

    def in_order(self, parts):
        rows = parts[0].shape[0]
        array = jnp.zeros((self.T * rows, *parts[0].shape[1:]), parts[0].dtype)
        for b, part in enumerate(parts):
            array = lax.dynamic_update_slice_in_dim(array, part, (self.corner ^ b) * rows, 0)
        return array

    def gather(self, block, own_parts, ready, sent=lambda: None):
        blocks = {0: block}
        if own_parts is not None:
            ready(0, own_parts)
        waiting = []
        order = [0, 1, 3, 2]
        for r in range(6):
            for k, parts in waiting:
                ready(k, parts + [self.swap(parts[1], self.near)])
            waiting = []
            if r == 5:
                return
            fresh = {}
            if r == 0:
                fresh[1] = self.shift(block, -1)
            elif r == 1:
                fresh[3] = self.shift(block, 1)
            elif r == 2:
                fresh["down"] = lax.ppermute(blocks[1], "slot", [(1, 0), (2, 1)])
                fresh["up"] = lax.ppermute(blocks[3], "slot", [(1, 2), (2, 3)])
            if r == 3:
                blocks[2] = lax.optimization_barrier(
                    jnp.where(self.s < 2, blocks["down"], blocks["up"])
                )
            if r < 4 and (r > 0 or own_parts is None):
                k = order[r]
                mine = blocks[k]
                parts = [mine, self.swap(mine, self.far), self.swap(mine, self.near)]
                fresh, parts = yield fresh, parts
                waiting = [(k, parts)]
            elif r < 4:
                (fresh,) = yield (fresh,)
            blocks.update(fresh)
            if r == 2:
                sent()

    def scatter(self, make, there, finish):
        order = [2, 1, 3, 0]
        near, far, from_two = {}, {}, {}
        got = []

        def total(k, *more):
            return lax.optimization_barrier(
                sum((a.astype(F32) for a in more), sum(a.astype(F32) for a in far[k])).astype(BF16)
            )

        for r in range(5):
            if r < 4:
                yield from until(lambda: there(order[r]))
            sent = {}
            if r >= 1:
                keep, give = near[order[r - 1]]
                away = (keep[1].astype(F32) + give[1].astype(F32)).astype(BF16)
                sent["far"] = (keep[0], give[0], self.swap(away, self.far))
            if r == 2:
                two = total(2)
                sent["up"] = lax.ppermute(two, "slot", [(0, 1), (1, 2)])
                sent["down"] = lax.ppermute(two, "slot", [(2, 1), (3, 2)])
            if r == 3:
                sent["got"] = self.shift(total(1, from_two["up"]), 1)
            if r == 4:
                sent["got"] = self.shift(total(3, from_two["down"]), -1)
            if r < 4:
                keep0, keep1, give0, give1 = make(order[r])
                sent["near"] = (
                    (keep0, keep1),
                    (self.swap(give0, self.near), self.swap(give1, self.near)),
                )
            sent, got = yield sent, got
            if "near" in sent:
                near[order[r]] = sent["near"]
            if "far" in sent:
                far[order[r - 1]] = sent["far"]
            if "up" in sent:
                from_two = sent
            if "got" in sent:
                got = got + [sent["got"]]
        finish(list(far[0]) + got)

    def ctx_before(self, block):
        C = self.C
        got = [
            lax.ppermute(block, "ctx", [(i, i + j) for i in range(C - j)])[None]
            for j in range(1, C)
        ]
        return got[0] if C == 2 else jnp.concatenate(got)

    def ctx_return(self, blocks):
        C = self.C
        got = [
            lax.ppermute(blocks[j - 1], "ctx", [(i, i - j) for i in range(j, C)])[None]
            for j in range(1, C)
        ]
        return got[0] if C == 2 else jnp.concatenate(got)

    def ctx_others(self, block):
        C = self.C
        return [
            lax.ppermute(block, "ctx", [(i, (i + j) % C) for i in range(C)]) for j in range(1, C)
        ]

    def gather_weights(self, pieces, done, sent, rounds):
        S, C = self.S, self.C
        d, wide = pieces[0].shape
        back = [(pieces[0], 0, 0)]
        blocks, starts = [], []
        rounds = list(rounds)
        while back or rounds:
            shifts = rounds.pop(0) if rounds else []
            parts = []
            for k, part in shifts:
                piece = pieces[k]
                if part is not None:
                    piece = piece[part * d // 2 : (part + 1) * d // 2]
                parts.append((piece, k, 0 if part is None else part * d // 2))
            got = [self.shift(piece, k) for piece, k, _ in parts]
            others = [self.ctx_others(block) for block, _, _ in back]
            got, others, blocks, pieces = yield got, others, blocks, pieces
            blocks = list(blocks)
            for (block, k, row), found in zip(back, others):
                for j, part in enumerate([block] + list(found)):
                    blocks.append(part)
                    starts.append((j, k, row))
            back = [(block, k, row) for block, (_, k, row) in zip(got, parts)]
            if not rounds:
                sent()
        j, k, row = jnp.asarray(starts, jnp.int32).T
        done(place(((self.c - j) % C * S + (self.s - k) % S) * d + row, blocks))

    def gather_weights_later(self, pieces, done, sent, steps):
        S, C = self.S, self.C
        d, wide = pieces[0].shape
        got = []
        for k, piece in ((1, pieces[1]), (3, pieces[3])) + self.halves(pieces[2]):
            got, pieces = yield got + [self.shift(piece, k)], pieces
        sent()
        k, row = jnp.asarray([(0, 0), (1, 0), (3, 0), (2, 0), (2, d // 2)], jnp.int32).T
        flat = place((self.s - k) % S * d + row, [pieces[0], *got])
        array = lax.all_gather(flat, "ctx")
        for _ in range(steps):
            yield ()
        done(array.reshape(C * S * d, wide))

    def halves(self, block):
        half = block.shape[0] // 2
        return ((2, block[:half]), (2, block[half:]))

    def scatter_weights(self, grad, done, steps):
        S, C = self.S, self.C
        wide = grad.shape[1]
        d = grad.shape[0] // (S * C)
        own = lax.psum_scatter(grad.reshape(C, S, d, wide), "ctx")
        for _ in range(steps):
            yield ()
        pieces = [
            lax.dynamic_index_in_dim(own, (self.s + k) % S, 0, keepdims=False) for k in range(S)
        ]
        got = []
        for k, piece in ((1, pieces[1]), (3, pieces[3])) + self.halves(pieces[2]):
            got, pieces = yield got + [self.shift(piece, k)], pieces
        done([pieces[0], got[0], jnp.concatenate(got[2:]), got[1]])

    def scatter_weights_now(self, grad, done, slow=False):
        S, C = self.S, self.C
        wide = grad.shape[1]
        d = grad.shape[0] // (S * C)
        grad = grad.reshape(C, S, d, wide)

        def piece(k, j):
            at = ((self.c + j) % C, (self.s + k) % S, 0, 0)
            return lax.dynamic_slice(grad, at, (1, 1, d, wide)).reshape(d, wide)

        def add(k):
            other = [
                lax.ppermute(piece(k, j), "ctx", [(i, (i + j) % C) for i in range(C)])
                for j in range(1, C)
            ]
            return [piece(k, 0)] + other

        def total(parts):
            value = sum((part.astype(F32) for part in parts[1:]), parts[0].astype(F32))
            return lax.optimization_barrier(value.astype(BF16))

        if slow:
            two, one = yield add(2), add(1)
            low, high = self.halves(total(two))
            low, high, one, three = yield self.shift(low[1], 2), high[1], one, add(3)
            low, high, one, three, own = yield low, self.shift(high, 2), one, three, add(0)
            low, high, one, three, own = yield low, high, self.shift(total(one), 1), three, own
            low, high, one, three, own = yield (
                low, high, one, self.shift(total(three), 3), total(own),
            )
            done([own, one, jnp.concatenate([low, high]), three])
            return
        two, one = yield add(2), add(1)
        two, one, three, own = yield self.shift(total(two), 2), self.shift(total(one), 1), add(3), add(0)
        two, one, three, own = yield two, one, self.shift(total(three), 3), total(own)
        done([own, one, two, three])

    def add_up(self, small, part, finish):
        cut = small.shape[0]
        both = jnp.concatenate([small, part])
        got = [self.shift(both, k) for k in range(1, self.S)]
        got, both = yield got, both
        both = sum(got, both)
        got = self.ctx_others(both)
        got, both = yield got, both
        both = sum(got, both)
        small, part = both[:cut], both[cut:]
        got = [self.swap(small, bit) for bit in range(1, self.T)]
        got, small, part = yield got, small, part
        finish(sum(got, small), part)


def on_device(
    inputs,
    lengths,
    ln_gain,
    ln_shift,
    w_qkv,
    b_qkv,
    w_out,
    b_out,
    w_up,
    b_up,
    w_down,
    b_down,
    cotangent,
):
    grp = Group()
    S, C, T = grp.S, grp.C, grp.T
    _, run, width = inputs.shape
    rows = run // T
    nt, ft = w_qkv.shape[3], w_up.shape[2]
    n, f = nt // S, ft // S
    d = w_up.shape[1]
    block = run // 2
    stages = Stages(lengths)

    here = jnp.concatenate([grp.c[None], grp.corner[None], lengths]).astype(jnp.int32)
    own_at = jnp.concatenate([(grp.c * run + grp.corner * rows)[None], lengths]).astype(jnp.int32)
    local = jnp.arange(run, dtype=jnp.int32)
    positions = grp.c * run + (local // rows ^ grp.corner) * rows + local % rows
    tables = rotary_tables(positions, n // HD)
    box = {}
    kept = [[None] * S for _ in range(LAYERS)]
    normed = [[None] * S for _ in range(LAYERS)]
    grad_branch = [[None] * S for _ in range(LAYERS)]
    middle = [[None] * S for _ in range(LAYERS)]
    gins = [[None] * S for _ in range(LAYERS)]
    bias_sums = [[None] * S for _ in range(LAYERS)]
    small_sums = [None] * LAYERS

    def bias_part(bias, size):
        return lax.dynamic_slice_in_dim(bias, grp.s * size, size, bias.ndim - 1)

    biases = [
        jnp.concatenate([bias_part(b_qkv[layer], n).reshape(-1), bias_part(b_up[layer], f)])[None]
        for layer in range(LAYERS)
    ]
    def after(*keys):
        return until(lambda: all(key in box for key in keys))

    def mark(*key):
        return lambda *value: box.__setitem__(key, value[0] if value else True)

    def lengths_of_all():
        got = yield [grp.shift(lengths, -k) for k in range(1, S)]
        for k, value in enumerate([lengths] + list(got)):
            box["at", k] = jnp.concatenate([value, grp.c[None], grp.corner[None]])

    def in_weights(layer, *keys, later=None):
        yield from after(*keys)
        pieces = pack(
            pack_in_kernel, grp.slot_at, w_qkv, w_up, layer, (d, 3 * n + f), S
        )
        pieces = list(stages.hold(*pieces))
        if later is None:
            yield from grp.gather_weights(
                pieces, mark("win", layer), mark("win sent", layer), FAST if layer == 0 else SLOW
            )
        else:
            yield from grp.gather_weights_later(
                pieces, mark("win", layer), mark("win sent", layer), later
            )

    def out_weights(layer, *keys, later=None):
        yield from after(*keys)
        pieces = pack(pack_out_kernel, grp.slot_at, w_out, w_down, layer, (d, n + f), S)
        pieces = list(stages.hold(*pieces))
        if later is None:
            yield from grp.gather_weights(
                pieces, mark("wout", layer), mark("wout sent", layer), FAST if layer == 0 else SLOW
            )
        else:
            yield from grp.gather_weights_later(
                pieces, mark("wout", layer), mark("wout sent", layer), later
            )

    def forward_slot(layer, k, parts):
        yield from after(("win", layer), ("at", k))
        normed[layer][k] = parts
        q, kv, up, act = in_project(parts, box["win", layer], biases[layer], tables, n)
        prev = grp.ctx_before(kv)
        if k != 2:
            q, kv, up, act = yield q, kv, up, act
        else:
            yield ()
        if k != 2:
            yield ()
        res, att, lse = attend(box["at", k], q, kv, prev, block, rows)
        box["attended", layer, k] = True
        kept[layer][k] = (q, kv, prev, up, act, res, att, lse)

    def make_forward(layer):
        def make(k):
            return out_project(kept[layer][k][6], kept[layer][k][4], box["wout", layer], rows)

        return make

    def there_forward(layer):
        return lambda k: ("attended", layer, k) in box and ("wout", layer) in box

    def backward_slot(layer, k, parts):
        yield from after(("wout", layer), ("attended", layer, k))
        grad_branch[layer][k] = parts
        if all(grad_branch[layer]):
            box["grad gathered", layer] = True
        q, kv, prev, up, _, res, _, lse = kept[layer][k]
        gatt, gup = out_back(parts, box["wout", layer], up, n)
        gq, gkv, gprev = attend_back(
            box["at", k], q, kv, prev, gatt, res, lse, tables, block, rows
        )
        if k == 2:
            got = grp.ctx_return(gprev)
            gq, gkv, gup = yield gq, gkv, gup
        else:
            gq, gkv, gup, gprev = yield gq, gkv, gup, gprev
            gq, gkv, gup, got = yield gq, gkv, gup, grp.ctx_return(gprev)
        middle[layer][k] = (gq, gkv, got, gup)
        box["middle", layer, k] = True

    def make_backward(layer):
        def make(k):
            gq, gkv, got, gup = middle[layer][k]
            gin, bias_sum, *parts = in_back(gq, gkv, got, gup, box["win", layer], tables, rows)
            gins[layer][k] = gin
            bias_sums[layer][k] = bias_sum[0]
            box["gin", layer, k] = True
            return parts

        return make

    def there_backward(layer):
        return lambda k: ("middle", layer, k) in box

    def slot_ready(kind, layer):
        return lambda m, parts: stages.spawn(kind(layer, m, parts))

    def rest_grads(layer, *keys, steps=4):
        yield from after(*keys)
        grad = weight_grad(
            [
                (
                    [part for parts in grad_branch[layer] for part in parts],
                    [[kept[layer][k][6] for k in range(S)], [kept[layer][k][4] for k in range(S)]],
                ),
                (
                    [part for parts in normed[layer] for part in parts],
                    [[middle[layer][k][3] for k in range(S)]],
                ),
            ],
            block,
        )
        yield ()
        if layer == 0:
            yield from grp.scatter_weights_now(grad, mark("grad rest", layer), slow=True)
        else:
            yield from grp.scatter_weights(grad, mark("grad rest", layer), steps)

    def qkv_grads(layer, steps=4):
        yield from after(*[("gin", layer, k) for k in range(S)])
        grad = weight_grad(
            [([part for parts in normed[layer] for part in parts], [gins[layer]])], block
        )
        (grad,) = yield (grad,)
        if layer == 0:
            yield from grp.scatter_weights_now(grad, mark("grad qkv", layer))
        else:
            yield from grp.scatter_weights(grad, mark("grad qkv", layer), steps)

    def first_gather(*keys):
        yield from after(*keys)
        box["hidden", 0], *parts = first_norm(here, inputs, ln_gain[0], ln_shift[0], S, C, T)
        parts = list(stages.hold(*parts))
        yield from grp.gather(
            parts[0], parts, slot_ready(forward_slot, 0), mark("normed sent", 0)
        )

    def next_gather(layer):
        yield from after(("hidden", layer))
        yield from grp.gather(
            box["normed", layer], None, slot_ready(forward_slot, layer), mark("normed sent", layer)
        )

    def forward_sum(layer, *keys):
        yield from after(*keys)

        def finish(parts):
            later = min(layer + 1, LAYERS - 1)
            box["hidden", layer + 1], box["normed", layer + 1] = sum_norm(
                parts,
                box["hidden", layer],
                (b_out[layer], b_down[layer], ln_gain[later], ln_shift[later]),
                S,
                C,
            )

        yield from grp.scatter(make_forward(layer), there_forward(layer), finish)

    def last_gradient(*keys):
        yield from after(*keys)
        box["grad", LAYERS], *parts = last_grad(here, cotangent, S, C, T)
        parts = list(stages.hold(*parts))
        yield from grp.gather(
            parts[0], parts, slot_ready(backward_slot, LAYERS - 1), mark("grad sent", LAYERS)
        )

    def next_gradient(layer):
        yield from after(("grad", layer))
        yield from grp.gather(
            box["grad low", layer],
            None,
            slot_ready(backward_slot, layer - 1),
            mark("grad sent", layer),
        )

    def backward_sum(layer):
        def finish(parts):
            box["grad", layer], box["grad low", layer], small_sums[layer] = sum_norm_back(
                parts, box["hidden", layer], box["grad", layer + 1], ln_gain[layer], S, C
            )

        yield from grp.scatter(make_backward(layer), there_backward(layer), finish)

    def all_sums(*keys):
        yield from after(*keys)
        spread = []
        for layer in range(LAYERS):
            total = sum(bias_sums[layer][1:], bias_sums[layer][0])
            pieces = jnp.zeros((3 * nt + ft,), F32)
            for i in range(3):
                pieces = lax.dynamic_update_slice_in_dim(
                    pieces, total[i * n : (i + 1) * n], i * nt + grp.s * n, 0
                )
            spread.append(
                lax.dynamic_update_slice_in_dim(pieces, total[3 * n :], 3 * nt + grp.s * f, 0)
            )
        yield from grp.add_up(
            jnp.concatenate(small_sums).reshape(-1),
            jnp.concatenate(spread),
            lambda small, part: box.__setitem__("sums", (small, part)),
        )

    def all_rows(key, value, name):
        yield from after(key)
        block = value()
        parts = [block, grp.swap(block, grp.far), grp.swap(block, grp.near)]
        parts = yield parts
        parts = list(parts) + [grp.swap(parts[1], grp.near)]
        starts = (grp.corner ^ jnp.arange(T, dtype=jnp.int32)) * rows
        box[name] = place(starts, parts)[None]

    def final_qkv(layer, *keys):
        yield from after(("grad qkv", layer), *keys)
        box["final qkv", layer] = unpack(
            unpack_qkv_kernel,
            grp.slot_at,
            box["grad qkv", layer],
            layer,
            ((LAYERS, 3, d, nt),),
            box.get(("final qkv", layer + 1)),
        )

    def final_rest(layer, *keys):
        yield from after(("grad rest", layer), *keys)
        box["final rest", layer] = unpack(
            unpack_rest_kernel,
            grp.slot_at,
            box["grad rest", layer],
            layer,
            ((LAYERS, nt, d), (LAYERS, ft, d), (LAYERS, d, ft)),
            box.get(("final rest", layer + 1)),
        )

    last = LAYERS - 1
    stages.spawn(in_weights(0))
    stages.spawn(lengths_of_all())
    stages.spawn(first_gather(("win sent", 0)))
    stages.spawn(forward_sum(0))
    stages.spawn(out_weights(0, ("normed sent", 0)))
    for layer in range(1, LAYERS):
        stages.spawn(in_weights(layer, ("wout sent", layer - 1)))
        stages.spawn(next_gather(layer))
        if layer < last:
            stages.spawn(forward_sum(layer))
        stages.spawn(out_weights(layer, ("win sent", layer)))
    stages.spawn(last_gradient(("normed sent", last)))
    for layer in reversed(range(LAYERS)):
        stages.spawn(backward_sum(layer))
        if layer > 0:
            stages.spawn(next_gradient(layer))
    stages.spawn(forward_sum(last, ("normed sent", last)))
    for layer in reversed(range(LAYERS)):
        stages.spawn(rest_grads(layer, ("gin", layer, 0 if layer else 1)))
        stages.spawn(qkv_grads(layer))
        stages.spawn(final_qkv(layer, *([] if layer == last else [("final qkv", layer + 1)])))
        stages.spawn(final_rest(layer, *([] if layer == last else [("final rest", layer + 1)])))
    stages.spawn(
        all_rows(
            ("hidden", LAYERS), lambda: rows_out(own_at, box["hidden", LAYERS], S, C), "block out"
        )
    )
    stages.spawn(all_rows(("grad", 0), lambda: rows_out(own_at, box["grad low", 0], S, C), "grad input"))
    stages.spawn(all_sums(("grad", 0)))
    stages.run()

    small, part = box["sums"]
    small = small.reshape(LAYERS, 3, width)
    part = part.reshape(LAYERS, 3 * nt + ft)
    (grad_qkv,) = box["final qkv", 0]
    grad_out, grad_down, grad_up = box["final rest", 0]
    return (
        box["block out"],
        box["grad input"],
        small[:, 0],
        small[:, 1],
        grad_qkv,
        part[:, : 3 * nt].reshape(LAYERS, 3, nt),
        grad_out,
        small[:, 2],
        grad_up,
        part[:, 3 * nt :],
        grad_down,
        small[:, 2],
    )


def solution(mesh):
    return jax.shard_map(
        on_device,
        mesh=mesh,
        in_specs=(
            P("slot", "ctx", None),
            P("slot"),
            P(),
            P(),
            P(None, None, ("slot", "ctx"), "tp"),
            P(None, None, "tp"),
            P(None, "tp", ("slot", "ctx")),
            P(),
            P(None, ("slot", "ctx"), "tp"),
            P(None, "tp"),
            P(None, "tp", ("slot", "ctx")),
            P(),
            P("slot", "ctx", None),
        ),
        out_specs=(
            P("slot", "ctx", None),
            P("slot", "ctx", None),
            P(),
            P(),
            P(None, None, ("slot", "ctx"), "tp"),
            P(None, None, "tp"),
            P(None, "tp", ("slot", "ctx")),
            P(),
            P(None, ("slot", "ctx"), "tp"),
            P(None, "tp"),
            P(None, "tp", ("slot", "ctx")),
            P(),
        ),
        check_vma=False,
    )
```
